512 devices in a mesh: grp: 8 (over z_lo), gy: 8 (over y, core), gx: 8 (over x, z_hi).
Axes of the slice: x: 4, y: 4, z: 16 (z_hi: 2, z_lo: 8; z = z_hi * 8 + z_lo), core: 2. Of those that a mesh axis runs over, the one named last changes fastest.
Arguments:
- right_side: float32 [64, 256, 1024], P('grp', 'gy', 'gx'), may hold values from -60 to 60
- reaction: float32 [64, 256, 1024], P('grp', 'gy', 'gx'), may hold values from 0.25 to 4
Outputs:
- correction: float32 [64, 256, 1024], P('grp', 'gy', 'gx')
- new_residual: float32 [64, 256, 1024], P('grp', 'gy', 'gx')
The draws below stay inside these ranges and needn't reach their ends.
All inputs are finite; a program needn't handle non-finite values.
Results may differ from the reference program's by a relative error of at most 0.000072.
Values sent between devices are 32-bit elements; how exact they have to be, the bound alone decides.
A program may use at most 64 MiB of HBM per device.

```python
import math
import jax
import jax.numpy as jnp

NZ = 64
NY = 256
NX = 1024


def draw_right_side(key, part):
    key = jax.random.fold_in(key, 7)
    rough_key, phase_key = jax.random.split(key)
    phases = jax.random.uniform(phase_key, (3,), jnp.float32, 0.0, 2.0 * math.pi)
    plane_coord = jnp.arange(NZ, dtype=jnp.float32)[:, None, None]
    row_coord = jnp.arange(NY, dtype=jnp.float32)[None, :, None]
    column_coord = jnp.arange(NX, dtype=jnp.float32)[None, None, :]
    smooth_wave = jnp.sin(2.0 * math.pi * (plane_coord + 0.5) / NZ + phases[0])
    smooth_wave = smooth_wave * jnp.sin(2.0 * math.pi * (row_coord + 0.5) / NY + phases[1])
    smooth_wave = smooth_wave * jnp.sin(2.0 * math.pi * (column_coord + 0.5) / NX + phases[2])
    rough = 12.0 * jax.random.truncated_normal(rough_key, -4.0, 4.0, (NZ, NY, NX), jnp.float32)
    smooth_part = 12.0 * smooth_wave
    return (rough + smooth_part).astype(jnp.float32)


def block_levels(key, dims, shards, low, high):
    gain, own = 1.0, jax.random.fold_in(key, 6)
    for position, shards_of in shards:
        heights = jnp.exp(jax.random.uniform(jax.random.fold_in(own, position), (shards_of,), jnp.float32, low / len(shards), high / len(shards)))
        gain = gain * jnp.repeat(heights, dims[position] // shards_of).reshape([-1 if axis == position else 1 for axis in range(len(dims))])
    return gain


def setup_inputs(seed: int = 0) -> dict:
    seeds = jax.random.split(jax.random.key(seed), 3)
    right_side = draw_right_side(jax.random.fold_in(seeds[2], 71), 0)
    reaction = jnp.clip(jnp.exp(math.log(4.0) - 2.7725887 * jax.random.uniform(seeds[1], (NZ, NY, NX), jnp.float32) ** block_levels(seeds[1], (NZ, NY, NX), ((0, 8), (1, 8), (2, 8)), -0.2, 0.2)), 0.25, 4.0)
    return {"right_side": right_side, "reaction": reaction}


stencil_weights = (1.0, 0.5, 0.25)
stencil_center = 14.0
coarse_share = 0.5
chebyshev_taus = tuple(1.0 / (1.15 + 0.85 * math.cos((2 * number - 1) * math.pi / 6.0)) for number in (1, 2, 3))


def neighbour_sum(padded, shape):
    summed = jnp.zeros(shape, jnp.float32)
    for offset_z in range(3):
        for offset_y in range(3):
            for offset_x in range(3):
                distance = abs(offset_z - 1) + abs(offset_y - 1) + abs(offset_x - 1)
                if distance > 0:
                    summed = summed + stencil_weights[distance - 1] * padded[offset_z:offset_z + shape[0], offset_y:offset_y + shape[1], offset_x:offset_x + shape[2]]
    return summed


def operate(values, diagonal, padder):
    return diagonal * values - neighbour_sum(padder(values), values.shape)


def smooth(source, diagonal, padder):
    iterate = chebyshev_taus[0] * source / diagonal
    for number in (1, 2):
        residue = source - operate(iterate, diagonal, padder)
        iterate = iterate + chebyshev_taus[number] * residue / diagonal
    return iterate


def restrict_mean(values):
    planes, rows_y, rows_x = values.shape
    return values.reshape(planes // 2, 2, rows_y // 2, 2, rows_x // 2, 2).mean(axis=(1, 3, 5))


def prolong_copy(values):
    planes, rows_y, rows_x = values.shape
    spread = jnp.broadcast_to(values[:, None, :, None, :, None], (planes, 2, rows_y, 2, rows_x, 2))
    return spread.reshape(planes * 2, rows_y * 2, rows_x * 2)


def zero_pad(values):
    return jnp.pad(values, 1)


def reference(right_side, reaction):
    diagonal = stencil_center + reaction
    fine_part = smooth(right_side, diagonal, zero_pad)
    source_two = restrict_mean(right_side)
    coef_two = restrict_mean(reaction)
    level_two = smooth(source_two, stencil_center + coef_two, zero_pad)
    source_three = restrict_mean(source_two)
    coef_three = restrict_mean(coef_two)
    level_three = smooth(source_three, stencil_center + coef_three, zero_pad)
    source_four = restrict_mean(source_three)
    coef_four = restrict_mean(coef_three)
    level_four = smooth(source_four, stencil_center + coef_four, zero_pad)
    coarse = prolong_copy(level_two + prolong_copy(level_three + prolong_copy(level_four)))
    correction = fine_part + coarse_share * coarse
    new_residual = right_side - operate(correction, diagonal, zero_pad)
    return correction, new_residual
```

```python
import functools
import math

import jax
import jax.numpy as jnp
from jax import lax
from jax.experimental import pallas as pl
from jax.experimental.pallas import tpu as pltpu
from jax.sharding import PartitionSpec as P

MESH = pl.DeviceIdType.MESH
AXES = ("grp", "gy", "gx")
TAUS = tuple(1.0 / (1.15 + 0.85 * math.cos((2 * k - 1) * math.pi / 6.0)) for k in (1, 2, 3))
EXACT = lax.Precision.HIGHEST
LANES = 128
HALO = 3
DEPTH = (8, 4, 2, 1)
ROWS = (32, 16, 8, 4)
COLS = (128, 64, 32, 16)
SENT = (32, 16, 8, 8)
TALL = (48, 32, 24, 24)
LANE0 = (0, 0, 60, 84)
ROW0 = (0, 48, 48, 0)
MSG_ROWS = 80


def iota(shape, dim):
    return lax.broadcasted_iota(jnp.int32, shape, dim)


def put(cond, value, other):
    return jnp.where(cond, value, other)


def extended_plane(ext, level, a, z):
    if level < 3:
        return ext[level][a, z]
    tile = put(iota((8, LANES), 0) < 4, ext[3][a, z, 8:16], ext[3][a, z, 16:24])
    return jnp.concatenate([ext[3][a, z, 0:8], tile], axis=0)


def exchange(s_hbm, c_hbm, e1, e2, e3, e4, got, sums2, sums3, sums4, msg, in_sem, zs, zr, ys, yr, xs, xr):
    ext = (e1, e2, e3, e4)
    place = tuple(lax.axis_index(a) for a in AXES)
    count = tuple(lax.axis_size(a) for a in AXES)

    def exists(dim, step):
        if step > 0:
            return place[dim] < count[dim] - step
        return place[dim] >= -step

    def device(dim, step):
        return tuple(p + (step if i == dim else 0) for i, p in enumerate(place))

    peers = [(0, k) for k in (1, -1, 2, -2, 3, -3)] + [(1, 1), (1, -1), (2, 1), (2, -1)]
    barrier = pltpu.get_barrier_semaphore()
    for dim, step in reversed(peers):

        @pl.when(exists(dim, step))
        def _():
            pl.semaphore_signal(barrier, inc=1, device_id=device(dim, step), device_id_type=MESH)

    loads = []
    for a, ref in enumerate((s_hbm, c_hbm)):
        load = pltpu.make_async_copy(ref, e1.at[a, 3:11, 8:40, :], in_sem.at[a])
        load.start()
        loads.append(load)
    for load in loads:
        load.wait()

    for a in range(2):
        for k in range(4):
            sums2[a, k] = sum(e1[a, 3 + 2 * k + dz, pl.ds(8 + dy, 16, stride=2), :] for dz in range(2) for dy in range(2))
        for k in range(2):
            sums3[a, k] = sum(sums2[a, 2 * k + dz, pl.ds(dy, 8, stride=2), :] for dz in range(2) for dy in range(2))
        deep = sum(sums3[a, dz, pl.ds(dy, 4, stride=2), :] for dz in range(2) for dy in range(2))
        sums4[a, 0, 0:4] = deep
        sums4[a, 0, 4:8] = deep
    for level, sums in ((1, sums2), (2, sums3), (3, sums4)):
        shape = sums.shape
        pick = jnp.where((iota((LANES, LANES), 0) >> level) == iota((LANES, LANES), 1), 0.125**level, 0.0)
        rows = sums[...].reshape(-1, LANES)
        mean = jnp.dot(rows, pick, precision=EXACT, preferred_element_type=jnp.float32).reshape(shape)
        d = DEPTH[level]
        ext[level][:, 3 : 3 + d, 8 : 8 + SENT[level], :] = mean

    expected = 0
    for dim, step in peers:
        expected = expected + jnp.where(exists(dim, step), 1, 0)
    pl.semaphore_wait(barrier, expected)

    def go(copies):
        for copy, to, _ in copies:
            pl.when(to)(copy.start)

    def landed(copies):
        for copy, _, fro in copies:
            pl.when(fro)(copy.wait_recv)

    def left(copies):
        for copy, to, _ in copies:
            pl.when(to)(copy.wait_send)

    copies = []
    for step in (1, -1, 2, -2, 3, -3):
        for level in range(4):
            d = DEPTH[level]
            if step > 0:
                first, last = max(0, step * d - HALO), d
            else:
                first, last = 0, min(d, HALO + step * d + d)
            if first >= last:
                continue
            at = 3 + first - step * d
            rows = slice(8, 8 + SENT[level])
            n = len(copies)
            copy = pltpu.make_async_remote_copy(
                src_ref=ext[level].at[:, 3 + first : 3 + last, rows, :],
                dst_ref=ext[level].at[:, at : at + last - first, rows, :],
                send_sem=zs.at[n],
                recv_sem=zr.at[n],
                device_id=device(0, step),
                device_id_type=MESH,
            )
            copies.append((copy, exists(0, step), exists(0, -step)))
    go(copies)
    landed(copies)
    sent = copies

    copies = []
    for step in (1, -1):
        for level in range(4):
            low, high, end = 8, SENT[level], 8 + SENT[level]
            src = high if step > 0 else low
            dst = 0 if step > 0 else end
            n = len(copies)
            copy = pltpu.make_async_remote_copy(
                src_ref=ext[level].at[:, :, src : src + 8, :],
                dst_ref=ext[level].at[:, :, dst : dst + 8, :],
                send_sem=ys.at[n],
                recv_sem=yr.at[n],
                device_id=device(1, step),
                device_id_type=MESH,
            )
            copies.append((copy, exists(1, step), exists(1, -step)))
    go(copies)
    landed(copies)
    sent = sent + copies

    for level in range(4):
        tall = 16 if level == 3 else TALL[level]
        lane = iota((tall, LANES), 1)
        packs = [jnp.zeros((tall, LANES), jnp.float32)] * 2
        for z in range(DEPTH[level] + 2 * HALO):
            for a in range(2):
                at = LANE0[level] + 6 * z + 3 * a
                here = (lane >= at) & (lane < at + 3)
                cells = extended_plane(ext, level, a, z)
                packs[0] = put(here, pltpu.roll(cells, at % LANES, 1), packs[0])
                packs[1] = put(here, pltpu.roll(cells, (at - COLS[level] + 3) % LANES, 1), packs[1])
        wide = 6 * (DEPTH[level] + 2 * HALO)
        here = (lane >= LANE0[level]) & (lane < LANE0[level] + wide)
        rows = slice(ROW0[level], ROW0[level] + tall)
        for side in range(2):
            if LANE0[level]:
                msg[side, rows] = put(here, packs[side], msg[side, rows])
            else:
                msg[side, rows] = packs[side]
    copies = []
    for side, step in ((0, -1), (1, 1)):
        copy = pltpu.make_async_remote_copy(
            src_ref=msg.at[side],
            dst_ref=got.at[1 - side],
            send_sem=xs.at[side],
            recv_sem=xr.at[side],
            device_id=device(2, step),
            device_id_type=MESH,
        )
        copies.append((copy, exists(2, step), exists(2, -step)))
    go(copies)
    landed(copies)
    left(sent + copies)


def ring_roll(chunks, shift):
    turned = [pltpu.roll(c, shift % LANES, 1) for c in chunks]
    if len(chunks) == 1:
        return turned
    lane = iota(chunks[0].shape, 1)
    edge = lane == (0 if shift > 0 else LANES - 1)
    return [put(edge, turned[1 - k], turned[k]) for k in range(2)]


def triple(planes, z):
    out = []
    for k in range(len(planes[z])):
        v = planes[z - 1][k] + 2.0 * planes[z][k] + planes[z + 1][k]
        n = v.shape[0]
        out.append(pltpu.roll(v, 1, 0) + 2.0 * v + pltpu.roll(v, n - 1, 0))
    before, after = ring_roll(out, 1), ring_roll(out, -1)
    return [b + 2.0 * v + f for b, v, f in zip(before, out, after)]


def cycle(e1, e2, e3, e4, got, corr_ref, res_ref, *spread):
    ext = (e1, e2, e3, e4)
    place = tuple(lax.axis_index(a) for a in AXES)
    count = tuple(lax.axis_size(a) for a in AXES)
    solved, sources, centres = [], [], []
    for level in range(4):
        d, rows, cols = DEPTH[level], ROWS[level], COLS[level]
        tall = 16 if level == 3 else TALL[level]
        lane, row = iota((tall, LANES), 1), iota((tall, LANES), 0)
        y = row - 8
        y_all = place[1] * rows + y
        y_ok = (y >= -HALO) & (y < rows + HALO) & (y_all >= 0) & (y_all < count[1] * rows)
        near = lane < cols
        right = (lane >= cols % LANES) & (lane < cols % LANES + HALO)
        leftward = lane >= LANES - HALO
        side_ok = (right & (place[2] < count[2] - 1)) | (leftward & (place[2] > 0))
        oks = [y_ok, y_ok & side_ok] if level == 0 else [y_ok & (near | side_ok)]
        src, cen, inv = [], [], []
        for z in range(d + 2 * HALO):
            z_all = place[0] * d + z - HALO
            z_ok = (z_all >= 0) & (z_all < count[0] * d)
            both = []
            for a in range(2):
                at = LANE0[level] + 6 * z + 3 * a
                strip = slice(ROW0[level], ROW0[level] + tall)
                main = extended_plane(ext, level, a, z)
                from_left = pltpu.roll(got[0, strip], (LANES - HALO - at) % LANES, 1)
                from_right = pltpu.roll(got[1, strip], (cols - at) % LANES, 1)
                if level == 0:
                    both.append([main, put(leftward, from_left, from_right)])
                else:
                    both.append([put(near, main, put(leftward, from_left, from_right))])
            oks_z = [ok & z_ok for ok in oks]
            src.append([put(ok, v, 0.0) for ok, v in zip(oks_z, both[0])])
            coef = [put(ok, v, 0.0) for ok, v in zip(oks_z, both[1])]
            cen.append([v + 16.0 for v in coef])
            inv.append([put(ok, 1.0 / (v + 14.0), 0.0) for ok, v in zip(oks_z, coef)])
        planes = [[TAUS[0] * s * i for s, i in zip(sz, iz)] for sz, iz in zip(src, inv)]
        for k in (1, 2):
            new = [None] * len(planes)
            for z in range(k, len(planes) - k):
                around = triple(planes, z)
                new[z] = [x + TAUS[k] * (s - m * x + 0.25 * t) * i for x, s, m, t, i in zip(planes[z], src[z], cen[z], around, inv[z])]
            planes = new
        solved.append(planes)
        sources.append(src)
        centres.append(cen)

    total = solved[3]
    for level in (2, 1, 0):
        tall = TALL[level]
        width = 2 * LANES if level == 0 else LANES
        col = iota((LANES, width), 1)
        col = put(col >= width - width // 4, col - width, col)
        pick = jnp.where(((col >> 1) & (LANES - 1)) == iota((LANES, width), 0), 1.0, 0.0)
        buf, wide = spread[2 * level], spread[2 * level + 1]
        coarse = DEPTH[level + 1]
        for n in range(coarse + 2):
            buf[n] = total[n + 2][0]
        for n in range(coarse + 2):
            half = buf[n, 4 : 4 + tall // 2, :]
            half = jnp.dot(half, pick, precision=EXACT, preferred_element_type=jnp.float32)
            for dy in range(2):
                for k in range(width // LANES):
                    wide[n, k, pl.ds(dy, tall // 2, stride=2), :] = half[:, k * LANES : (k + 1) * LANES]
        new = [None] * len(solved[level])
        share = 0.5 if level == 0 else 1.0
        for z in range(-1, DEPTH[level] + 1):
            n = (z >> 1) + 1
            new[z + 3] = [x + share * wide[n, k] for k, x in enumerate(solved[level][z + 3])]
        total = new
    for z in range(8):
        corr_ref[z] = total[z + 3][0][8:40]
        around = triple(total, z + 3)[0]
        res = sources[0][z + 3][0] - centres[0][z + 3][0] * total[z + 3][0] + 0.25 * around
        res_ref[z] = res[8:40]


def per_device(right_side, reaction):
    f32 = jnp.float32
    vmem = pl.BlockSpec(memory_space=pltpu.VMEM)
    shapes = [jax.ShapeDtypeStruct((2, d + 2 * HALO, t, LANES), f32) for d, t in zip(DEPTH, TALL)]
    shapes.append(jax.ShapeDtypeStruct((2, MSG_ROWS, LANES), f32))
    extended = pl.pallas_call(
        exchange,
        out_shape=shapes,
        in_specs=[pl.BlockSpec(memory_space=pl.ANY)] * 2,
        out_specs=[vmem] * 5,
        scratch_shapes=[
            pltpu.VMEM((2, 4, 16, LANES), f32),
            pltpu.VMEM((2, 2, 8, LANES), f32),
            pltpu.VMEM((2, 1, 8, LANES), f32),
            pltpu.VMEM((2, MSG_ROWS, LANES), f32),
            pltpu.SemaphoreType.DMA((2,)),
            pltpu.SemaphoreType.DMA((16,)),
            pltpu.SemaphoreType.DMA((16,)),
            pltpu.SemaphoreType.DMA((8,)),
            pltpu.SemaphoreType.DMA((8,)),
            pltpu.SemaphoreType.DMA((2,)),
            pltpu.SemaphoreType.DMA((2,)),
        ],
        compiler_params=pltpu.CompilerParams(collective_id=0, has_side_effects=True, vmem_limit_bytes=32 * 1024 * 1024),
    )(right_side, reaction)
    block = jax.ShapeDtypeStruct(right_side.shape, f32)
    spread = []
    for level in (0, 1, 2):
        coarse_tall = 16 if level == 2 else TALL[level + 1]
        n = DEPTH[level + 1] + 2
        spread.append(pltpu.VMEM((n, coarse_tall, LANES), f32))
        spread.append(pltpu.VMEM((n, 2 if level == 0 else 1, TALL[level], LANES), f32))
    return pl.pallas_call(
        cycle,
        out_shape=[block, block],
        in_specs=[vmem] * 5,
        out_specs=[vmem] * 2,
        scratch_shapes=spread,
        compiler_params=pltpu.CompilerParams(vmem_limit_bytes=32 * 1024 * 1024),
    )(*extended)


def solution(mesh):
    spec = P(*AXES)
    return jax.shard_map(
        lambda s, c: tuple(per_device(s, c)),
        mesh=mesh,
        in_specs=(spec, spec),
        out_specs=(spec, spec),
        check_vma=False,
    )
```

```python
import functools
import math

import jax
import jax.numpy as jnp
from jax import lax
from jax.experimental import pallas as pl
from jax.experimental.pallas import tpu as pltpu
from jax.sharding import PartitionSpec as P

MESH = pl.DeviceIdType.MESH
AXES = ("grp", "gy", "gx")
TAUS = tuple(1.0 / (1.15 + 0.85 * math.cos((2 * k - 1) * math.pi / 6.0)) for k in (1, 2, 3))
EXACT = lax.Precision.HIGHEST
LANES = 128
HALO = 3
DEPTH = (8, 4, 2, 1)
ROWS = (32, 16, 8, 4)
COLS = (128, 64, 32, 16)
TALL = (48, 32, 24, 16)
NEAR = tuple((dz, dy) for dz in (-1, 0, 1) for dy in (-1, 0, 1) if dz or dy)
FAR = tuple((dz, dy) for dz in (-3, 3, -2, 2) for dy in (-1, 0, 1))


def iota(shape, dim):
    return lax.broadcasted_iota(jnp.int32, shape, dim)


def put(cond, value, other):
    return jnp.where(cond, value, other)


def exchange(s_hbm, c_hbm, fine, second, deep, strips, sums2, sums3, sums4, msg, in_sem, xs, xr, bs, br, fs, fr):
    place = tuple(lax.axis_index(a) for a in AXES)
    count = tuple(lax.axis_size(a) for a in AXES)

    def exists(*steps):
        ok = True
        for p, n, step in zip(place, count, steps):
            if step > 0:
                ok = ok & (p < n - step)
            if step < 0:
                ok = ok & (p >= -step)
        return ok

    def device(*steps):
        return tuple(p + step for p, step in zip(place, steps))

    peers = [(0, 0, -1), (0, 0, 1)] + [(dz, dy, 0) for dz, dy in FAR + NEAR]
    barrier = pltpu.get_barrier_semaphore()
    for peer in peers:

        @pl.when(exists(*peer))
        def _():
            pl.semaphore_signal(barrier, inc=1, device_id=device(*peer), device_id_type=MESH)

    loads = []
    for a, ref in enumerate((s_hbm, c_hbm)):
        load = pltpu.make_async_copy(ref, fine.at[a, 3:11, 8:40, :], in_sem.at[a])
        load.start()
        loads.append(load)
    for load in loads:
        load.wait()

    for a in range(2):
        for k in range(4):
            sums2[a, k] = sum(fine[a, 3 + 2 * k + dz, pl.ds(8 + dy, 16, stride=2), :] for dz in range(2) for dy in range(2))
        for k in range(2):
            sums3[a, k] = sum(sums2[a, 2 * k + dz, pl.ds(dy, 8, stride=2), :] for dz in range(2) for dy in range(2))
        last = sum(sums3[a, dz, pl.ds(dy, 4, stride=2), :] for dz in range(2) for dy in range(2))
        sums4[a, 0:4] = last
        sums4[a, 4:8] = last

    def mean(level, rows, first):
        pick = jnp.where((iota((LANES, LANES), 0) >> level) + first == iota((LANES, LANES), 1), 0.125**level, 0.0)
        return jnp.dot(rows, pick, precision=EXACT, preferred_element_type=jnp.float32)

    level2 = sum(mean(1, sums2[a].reshape(64, LANES), 64 * a) for a in range(2))
    second[3:7, 8:24, :] = level2.reshape(4, 16, LANES)
    level3 = sum(mean(2, sums3[a].reshape(16, LANES), 32 * a) for a in range(2)).reshape(2, 8, LANES)
    level4 = sum(mean(3, sums4[a], 64 + 16 * a) for a in range(2))
    deep[3, 1] = level3 + level4[None]

    def gather(parts, rows):
        lane = iota((rows, LANES), 1)
        packs = [jnp.zeros((rows, LANES), jnp.float32)] * 2
        for cells, at, first, cols in parts:
            here = (lane >= at) & (lane < at + HALO)
            packs[0] = put(here, pltpu.roll(cells, (at - first) % LANES, 1), packs[0])
            packs[1] = put(here, pltpu.roll(cells, (at - first - cols + HALO) % LANES, 1), packs[1])
        return packs

    parts = []
    for a in range(2):
        for z in range(8):
            for half in range(2):
                cells = fine[a, 3 + z, 8 + 16 * half : 24 + 16 * half]
                parts.append((cells, 48 * half + 6 * z + 3 * a, 0, 128))
        for z in range(4):
            parts.append((second[3 + z, 8:24], 96 + 6 * z + 3 * a, 64 * a, 64))
    upper = gather(parts, 16)
    parts = []
    for a in range(2):
        for z in range(2):
            parts.append((deep[3, 1, z], 6 * z + 3 * a, 32 * a, 32))
        parts.append((deep[3, 1, 0], 12 + 3 * a, 64 + 16 * a, 16))
    lower = gather(parts, 8)
    for side in range(2):
        msg[side, 0:8] = upper[side][0:8]
        msg[side, 8:16] = lower[side]
        msg[side, 16:24] = upper[side][8:16]

    expected = 0
    for peer in peers:
        expected = expected + jnp.where(exists(*peer), 1, 0)
    pl.semaphore_wait(barrier, expected)

    def remote(src, dst, sems, n, *peer):
        copy = pltpu.make_async_remote_copy(
            src_ref=src, dst_ref=dst, send_sem=sems[0].at[n], recv_sem=sems[1].at[n], device_id=device(*peer), device_id_type=MESH
        )
        pl.when(exists(*peer))(copy.start)
        return copy, exists(*peer), exists(*(-step for step in peer))

    def landed(copies):
        for copy, _, fro in copies:
            pl.when(fro)(copy.wait_recv)

    across = [remote(msg.at[side], strips.at[3, 1, 1 - side], (xs, xr), side, 0, 0, 2 * side - 1) for side in range(2)]

    blocks = []
    for dz, dy in NEAR + FAR:
        for ref, depth, rows in ((fine, 8, 32), (second, 4, 16)):
            if abs(dz) > 1:
                continue
            z0, z1 = {-1: (3, 6), 0: (3, 3 + depth), 1: (depth, 3 + depth)}[dz]
            y0, y1 = {-1: (8, 16), 0: (8, 8 + rows), 1: (rows, 8 + rows)}[dy]
            up, along = z0 - dz * depth, y0 - dy * rows
            src, dst = ref, ref
            if ref is fine:
                src, dst = fine.at[:, z0:z1, y0:y1, :], fine.at[:, up : up + z1 - z0, along : along + y1 - y0, :]
            else:
                src, dst = second.at[z0:z1, y0:y1, :], second.at[up : up + z1 - z0, along : along + y1 - y0, :]
            blocks.append(remote(src, dst, (bs, br), len(blocks), dz, dy, 0))
        blocks.append(remote(deep.at[3, 1], deep.at[3 - dz, 1 - dy], (bs, br), len(blocks), dz, dy, 0))

    landed(across)
    passed = []
    for dz, dy in FAR + NEAR:
        rows = slice(8, 16) if abs(dz) > 1 else {-1: slice(0, 16), 0: slice(0, 24), 1: slice(8, 24)}[dy]
        passed.append(remote(strips.at[3, 1, :, rows, :], strips.at[3 - dz, 1 - dy, :, rows, :], (fs, fr), len(passed), dz, dy, 0))
    landed(blocks + passed)
    for copy, to, _ in across + blocks + passed:
        pl.when(to)(copy.wait_send)


def ring_roll(chunks, shift):
    turned = [pltpu.roll(c, shift % LANES, 1) for c in chunks]
    if len(chunks) == 1:
        return turned
    lane = iota(chunks[0].shape, 1)
    edge = lane == (0 if shift > 0 else LANES - 1)
    return [put(edge, turned[1 - k], turned[k]) for k in range(2)]


def triple(planes, z):
    out = []
    for k in range(len(planes[z])):
        v = planes[z - 1][k] + 2.0 * planes[z][k] + planes[z + 1][k]
        n = v.shape[0]
        out.append(pltpu.roll(v, 1, 0) + 2.0 * v + pltpu.roll(v, n - 1, 0))
    before, after = ring_roll(out, 1), ring_roll(out, -1)
    return [b + 2.0 * v + f for b, v, f in zip(before, out, after)]


def columns(strips, level, a, z, side, first):
    dz, p = z // DEPTH[level], z % DEPTH[level]

    def tiles(dy, lane, *which):
        rows = [strips[dz + 3, dy + 1, side, 8 * t : 8 * t + 8] for t in which]
        rows = rows[0] if len(rows) == 1 else jnp.concatenate(rows, axis=0)
        return pltpu.roll(rows, (first - lane) % LANES, 1)

    if level == 0:
        low, high = 6 * p + 3 * a, 48 + 6 * p + 3 * a
        pieces = [tiles(-1, high, 2), tiles(0, low, 0, 2), tiles(0, high, 0, 2), tiles(1, low, 0)]
    elif level == 1:
        at = 96 + 6 * p + 3 * a
        pieces = [tiles(-1, at, 2), tiles(0, at, 0, 2), tiles(1, at, 0)]
    else:
        at = 6 * p + 3 * a if level == 2 else 12 + 3 * a
        pieces = [tiles(dy, at, 1) for dy in (-1, 0, 1)]
        if level == 3:
            pieces = [pieces[0], put(iota((8, LANES), 0) < 4, pieces[1], pieces[2])]
    return jnp.concatenate(pieces, axis=0)


def own(fine, second, deep, level, a, z):
    if level == 0:
        return fine[a, z + 3]
    if level == 1:
        return pltpu.roll(second[z + 3], 64, 1) if a else second[z + 3]
    dz, p = z // DEPTH[level], z % DEPTH[level]
    pieces = [deep[dz + 3, dy, p] for dy in range(3)]
    if level == 3:
        pieces = [pieces[0], put(iota((8, LANES), 0) < 4, pieces[1], pieces[2])]
    cells = jnp.concatenate(pieces, axis=0)
    first = 32 * a if level == 2 else 64 + 16 * a
    return pltpu.roll(cells, (-first) % LANES, 1) if first else cells


def cycle(fine, second, deep, strips, corr_ref, res_ref, *spread):
    place = tuple(lax.axis_index(a) for a in AXES)
    count = tuple(lax.axis_size(a) for a in AXES)
    solved, sources, centres = [], [], []
    for level in range(4):
        d, rows, cols, tall = DEPTH[level], ROWS[level], COLS[level], TALL[level]
        lane, row = iota((tall, LANES), 1), iota((tall, LANES), 0)
        y = row - 8
        y_all = place[1] * rows + y
        y_ok = (y >= -HALO) & (y < rows + HALO) & (y_all >= 0) & (y_all < count[1] * rows)
        near = lane < cols
        right = (lane >= cols % LANES) & (lane < cols % LANES + HALO)
        leftward = lane >= LANES - HALO
        side_ok = (right & (place[2] < count[2] - 1)) | (leftward & (place[2] > 0))
        oks = [y_ok, y_ok & side_ok] if level == 0 else [y_ok & (near | side_ok)]
        src, cen, inv = [], [], []
        for z in range(-HALO, d + HALO):
            z_all = place[0] * d + z
            z_ok = (z_all >= 0) & (z_all < count[0] * d)
            both = []
            for a in range(2):
                main = own(fine, second, deep, level, a, z)
                sides = put(leftward, columns(strips, level, a, z, 0, LANES - HALO), columns(strips, level, a, z, 1, cols % LANES))
                both.append([main, sides] if level == 0 else [put(near, main, sides)])
            oks_z = [ok & z_ok for ok in oks]
            src.append([put(ok, v, 0.0) for ok, v in zip(oks_z, both[0])])
            coef = [put(ok, v, 0.0) for ok, v in zip(oks_z, both[1])]
            cen.append([v + 16.0 for v in coef])
            inv.append([put(ok, 1.0 / (v + 14.0), 0.0) for ok, v in zip(oks_z, coef)])
        planes = [[TAUS[0] * s * i for s, i in zip(sz, iz)] for sz, iz in zip(src, inv)]
        for k in (1, 2):
            new = [None] * len(planes)
            for z in range(k, len(planes) - k):
                around = triple(planes, z)
                new[z] = [x + TAUS[k] * (s - m * x + 0.25 * t) * i for x, s, m, t, i in zip(planes[z], src[z], cen[z], around, inv[z])]
            planes = new
        solved.append(planes)
        sources.append(src)
        centres.append(cen)

    total = solved[3]
    for level in (2, 1, 0):
        tall = TALL[level]
        width = 2 * LANES if level == 0 else LANES
        col = iota((LANES, width), 1)
        col = put(col >= width - width // 4, col - width, col)
        pick = jnp.where(((col >> 1) & (LANES - 1)) == iota((LANES, width), 0), 1.0, 0.0)
        buf, wide = spread[2 * level], spread[2 * level + 1]
        coarse = DEPTH[level + 1]
        for n in range(coarse + 2):
            buf[n] = total[n + 2][0]
        for n in range(coarse + 2):
            half = buf[n, 4 : 4 + tall // 2, :]
            half = jnp.dot(half, pick, precision=EXACT, preferred_element_type=jnp.float32)
            for dy in range(2):
                for k in range(width // LANES):
                    wide[n, k, pl.ds(dy, tall // 2, stride=2), :] = half[:, k * LANES : (k + 1) * LANES]
        new = [None] * len(solved[level])
        share = 0.5 if level == 0 else 1.0
        for z in range(-1, DEPTH[level] + 1):
            n = (z >> 1) + 1
            new[z + 3] = [x + share * wide[n, k] for k, x in enumerate(solved[level][z + 3])]
        total = new
    for z in range(8):
        corr_ref[z] = total[z + 3][0][8:40]
        around = triple(total, z + 3)[0]
        res = sources[0][z + 3][0] - centres[0][z + 3][0] * total[z + 3][0] + 0.25 * around
        res_ref[z] = res[8:40]


def per_device(right_side, reaction):
    f32 = jnp.float32
    vmem = pl.BlockSpec(memory_space=pltpu.VMEM)
    shapes = [(2, 14, 48, LANES), (10, 32, LANES), (7, 3, 2, 8, LANES), (7, 3, 2, 24, LANES)]
    dma = pltpu.SemaphoreType.DMA
    blocks = 3 * len(NEAR) + len(FAR)
    extended = pl.pallas_call(
        exchange,
        out_shape=[jax.ShapeDtypeStruct(shape, f32) for shape in shapes],
        in_specs=[pl.BlockSpec(memory_space=pltpu.HBM)] * 2,
        out_specs=[vmem] * 4,
        scratch_shapes=[
            pltpu.VMEM((2, 4, 16, LANES), f32),
            pltpu.VMEM((2, 2, 8, LANES), f32),
            pltpu.VMEM((2, 8, LANES), f32),
            pltpu.VMEM((2, 24, LANES), f32),
            dma((2,)),
            dma((2,)),
            dma((2,)),
            dma((blocks,)),
            dma((blocks,)),
            dma((20,)),
            dma((20,)),
        ],
        compiler_params=pltpu.CompilerParams(collective_id=0, has_side_effects=True, vmem_limit_bytes=16 * 1024 * 1024),
    )(right_side, reaction)
    block = jax.ShapeDtypeStruct(right_side.shape, f32)
    spread = []
    for level in (0, 1, 2):
        n = DEPTH[level + 1] + 2
        spread.append(pltpu.VMEM((n, TALL[level + 1], LANES), f32))
        spread.append(pltpu.VMEM((n, 2 if level == 0 else 1, TALL[level], LANES), f32))
    return pl.pallas_call(
        cycle,
        out_shape=[block, block],
        in_specs=[vmem] * 4,
        out_specs=[vmem] * 2,
        scratch_shapes=spread,
        compiler_params=pltpu.CompilerParams(vmem_limit_bytes=16 * 1024 * 1024),
    )(*extended)


def solution(mesh):
    spec = P(*AXES)
    return jax.shard_map(
        lambda s, c: tuple(per_device(s, c)),
        mesh=mesh,
        in_specs=(spec, spec),
        out_specs=(spec, spec),
        check_vma=False,
    )
```

```python
import functools
import math

import jax
import jax.numpy as jnp
from jax import lax
from jax.experimental import pallas as pl
from jax.experimental.pallas import tpu as pltpu
from jax.sharding import PartitionSpec as P

MESH = pl.DeviceIdType.MESH
AXES = ("grp", "gy", "gx")
TAUS = tuple(1.0 / (1.15 + 0.85 * math.cos((2 * k - 1) * math.pi / 6.0)) for k in (1, 2, 3))
EXACT = lax.Precision.HIGHEST
LANES = 128
HALO = 3
DEPTH = (8, 4, 2, 1)
ROWS = (32, 16, 8, 4)
COLS = (128, 64, 32, 16)
TALL = (48, 32, 24, 16)
NEAR = tuple((dz, dy) for dz in (-1, 0, 1) for dy in (-1, 0, 1) if dz or dy)
FAR = tuple((dz, dy) for dz in (-3, 3, -2, 2) for dy in (-1, 0, 1))


def iota(shape, dim):
    return lax.broadcasted_iota(jnp.int32, shape, dim)


def put(cond, value, other):
    return jnp.where(cond, value, other)


def slide(cells, width):
    row = iota(cells.shape, 0)
    for k in (1, 2, 4):
        cells = put(row & k != 0, pltpu.roll(cells, k * width % LANES, 1), cells)
    return cells


def in_row(cells, width):
    return jnp.sum(slide(cells, width), axis=0, keepdims=True)


def off_row(row, width):
    return slide(jnp.broadcast_to(row, (8, LANES)), LANES - width)


def exchange(s_hbm, c_hbm, fine, second, deep, strips, sums2, sums3, sums4, msg, in_sem, xs, xr, bs, br, fs, fr):
    place = tuple(lax.axis_index(a) for a in AXES)
    count = tuple(lax.axis_size(a) for a in AXES)

    def exists(*steps):
        ok = True
        for p, n, step in zip(place, count, steps):
            if step > 0:
                ok = ok & (p < n - step)
            if step < 0:
                ok = ok & (p >= -step)
        return ok

    def device(*steps):
        return tuple(p + step for p, step in zip(place, steps))

    peers = [(0, 0, -1), (0, 0, 1)] + [(dz, dy, 0) for dz, dy in FAR + NEAR]
    barrier = pltpu.get_barrier_semaphore()
    for peer in peers:

        @pl.when(exists(*peer))
        def _():
            pl.semaphore_signal(barrier, inc=1, device_id=device(*peer), device_id_type=MESH)

    loads = []
    for a, ref in enumerate((s_hbm, c_hbm)):
        load = pltpu.make_async_copy(ref, fine.at[a, 3:11, 8:40, :], in_sem.at[a])
        load.start()
        loads.append(load)
    for load in loads:
        load.wait()

    for a in range(2):
        for k in range(4):
            sums2[a, k] = sum(fine[a, 3 + 2 * k + dz, pl.ds(8 + dy, 16, stride=2), :] for dz in range(2) for dy in range(2))
        for k in range(2):
            sums3[a, k] = sum(sums2[a, 2 * k + dz, pl.ds(dy, 8, stride=2), :] for dz in range(2) for dy in range(2))
        last = sum(sums3[a, dz, pl.ds(dy, 4, stride=2), :] for dz in range(2) for dy in range(2))
        sums4[a, 0:4] = last
        sums4[a, 4:8] = jnp.zeros_like(last)

    def mean(level, rows, first):
        pick = jnp.where((iota((LANES, LANES), 0) >> level) + first == iota((LANES, LANES), 1), 0.125**level, 0.0)
        return jnp.dot(rows, pick, precision=EXACT, preferred_element_type=jnp.float32)

    level2 = sum(mean(1, sums2[a].reshape(64, LANES), 64 * a) for a in range(2))
    second[3:7, 8:24, :] = level2.reshape(4, 16, LANES)
    level3 = sum(mean(2, sums3[a, z], 64 * z + 32 * a) for a in range(2) for z in range(2))
    level4 = in_row(sum(mean(3, sums4[a], 16 * a) for a in range(2)), 32)
    deep[3, 1, 0:8] = level3
    deep[3, 1, 8:9] = level4

    def gather(parts, rows):
        lane = iota((rows, LANES), 1)
        packs = [jnp.zeros((rows, LANES), jnp.float32)] * 2
        for cells, at, first, cols in parts:
            here = (lane >= at) & (lane < at + HALO)
            packs[0] = put(here, pltpu.roll(cells, (at - first) % LANES, 1), packs[0])
            packs[1] = put(here, pltpu.roll(cells, (at - first - cols + HALO) % LANES, 1), packs[1])
        return packs

    parts = []
    for a in range(2):
        for z in range(8):
            for half in range(2):
                cells = fine[a, 3 + z, 8 + 16 * half : 24 + 16 * half]
                parts.append((cells, 48 * half + 6 * z + 3 * a, 0, 128))
        for z in range(4):
            parts.append((second[3 + z, 8:24], 96 + 6 * z + 3 * a, 64 * a, 64))
    upper = gather(parts, 16)
    parts = []
    for a in range(2):
        for z in range(2):
            parts.append((level3, 6 * z + 3 * a, 64 * z + 32 * a, 32))
    lower = gather(parts, 8)
    last = off_row(level4, 32)
    last = gather([(last, 3 * a, 16 * a, 16) for a in range(2)], 8)
    for side in range(2):
        msg[side, 0:8] = upper[side][8:16]
        msg[side, 8:9] = in_row(lower[side], 16)
        msg[side, 9:10] = in_row(last[side], 16)
        msg[side, 10:18] = upper[side][0:8]

    expected = 0
    for peer in peers:
        expected = expected + jnp.where(exists(*peer), 1, 0)
    pl.semaphore_wait(barrier, expected)

    def remote(src, dst, sems, n, *peer):
        copy = pltpu.make_async_remote_copy(
            src_ref=src, dst_ref=dst, send_sem=sems[0].at[n], recv_sem=sems[1].at[n], device_id=device(*peer), device_id_type=MESH
        )
        pl.when(exists(*peer))(copy.start)
        return copy, exists(*peer), exists(*(-step for step in peer))

    def landed(copies):
        for copy, _, fro in copies:
            pl.when(fro)(copy.wait_recv)

    across = [remote(msg.at[side, 0:18], strips.at[3, 1, 1 - side, 0:18], (xs, xr), side, 0, 0, 2 * side - 1) for side in range(2)]

    blocks = []
    for dz, dy in NEAR + FAR:
        for ref, depth, rows in ((fine, 8, 32), (second, 4, 16)):
            if abs(dz) > 1:
                continue
            z0, z1 = {-1: (3, 6), 0: (3, 3 + depth), 1: (depth, 3 + depth)}[dz]
            y0, y1 = {-1: (8, 11), 0: (8, 8 + rows), 1: (rows + 5, rows + 8)}[dy]
            up, along = z0 - dz * depth, y0 - dy * rows
            src, dst = ref, ref
            if ref is fine:
                src, dst = fine.at[:, z0:z1, y0:y1, :], fine.at[:, up : up + z1 - z0, along : along + y1 - y0, :]
            else:
                src, dst = second.at[z0:z1, y0:y1, :], second.at[up : up + z1 - z0, along : along + y1 - y0, :]
            blocks.append(remote(src, dst, (bs, br), len(blocks), dz, dy, 0))
        rows = slice(8, 9) if abs(dz) == 3 else slice(0, 9)
        blocks.append(remote(deep.at[3, 1, rows], deep.at[3 - dz, 1 - dy, rows], (bs, br), len(blocks), dz, dy, 0))

    landed(across)
    passed = []
    for dz, dy in FAR + NEAR:
        rows = slice(8, 10) if abs(dz) > 1 else {-1: slice(8, 13), 0: slice(0, 18), 1: slice(5, 10)}[dy]
        passed.append(remote(strips.at[3, 1, :, rows, :], strips.at[3 - dz, 1 - dy, :, rows, :], (fs, fr), len(passed), dz, dy, 0))
    landed(blocks + passed)
    for copy, to, _ in across + blocks + passed:
        pl.when(to)(copy.wait_send)


def ring_roll(chunks, shift):
    turned = [pltpu.roll(c, shift % LANES, 1) for c in chunks]
    if len(chunks) == 1:
        return turned
    lane = iota(chunks[0].shape, 1)
    edge = lane == (0 if shift > 0 else LANES - 1)
    return [put(edge, turned[1 - k], turned[k]) for k in range(2)]


def triple(planes, z):
    out = []
    for k in range(len(planes[z])):
        v = planes[z - 1][k] + 2.0 * planes[z][k] + planes[z + 1][k]
        n = v.shape[0]
        out.append(pltpu.roll(v, 1, 0) + 2.0 * v + pltpu.roll(v, n - 1, 0))
    before, after = ring_roll(out, 1), ring_roll(out, -1)
    return [b + 2.0 * v + f for b, v, f in zip(before, out, after)]


def columns(strips, level, a, z, side, first, seen):
    dz, p = z // DEPTH[level], z % DEPTH[level]

    def tiles(dy, lane, *which):
        rows = [strips[dz + 3, dy + 1, side, 10:18] if t == 0 else strips[dz + 3, dy + 1, side, 0:8] for t in which]
        rows = rows[0] if len(rows) == 1 else jnp.concatenate(rows, axis=0)
        return pltpu.roll(rows, (first - lane) % LANES, 1)

    if level == 0:
        low, high = 6 * p + 3 * a, 48 + 6 * p + 3 * a
        pieces = [tiles(-1, high, 1), tiles(0, low, 0, 1), tiles(0, high, 0, 1), tiles(1, low, 0)]
    elif level == 1:
        at = 96 + 6 * p + 3 * a
        pieces = [tiles(-1, at, 1), tiles(0, at, 0, 1), tiles(1, at, 0)]
    else:
        pieces = []
        for dy in range(3):
            key = (level, dz, dy, side)
            if key not in seen:
                seen[key] = off_row(strips[dz + 3, dy, side, level + 6 : level + 7], 16)
            cells = seen[key]
            pieces.append(pltpu.roll(cells, (first - 6 * p - 3 * a) % LANES, 1))
        if level == 3:
            pieces = [pieces[0], put(iota((8, LANES), 0) < 4, pieces[1], pieces[2])]
    return jnp.concatenate(pieces, axis=0)


def own(fine, second, deep, level, a, z, seen):
    if level == 0:
        return fine[a, z + 3]
    if level == 1:
        return pltpu.roll(second[z + 3], 64, 1) if a else second[z + 3]
    dz, p = z // DEPTH[level], z % DEPTH[level]
    if level == 2:
        return pltpu.roll(jnp.concatenate([deep[dz + 3, dy, 0:8] for dy in range(3)], axis=0), (-64 * p - 32 * a) % LANES, 1)
    if z not in seen:
        seen[z] = [off_row(deep[dz + 3, dy, 8:9], 32) for dy in range(3)]
    pieces = seen[z]
    pieces = [pieces[0], put(iota((8, LANES), 0) < 4, pieces[1], pieces[2])]
    return pltpu.roll(jnp.concatenate(pieces, axis=0), (-16 * a) % LANES, 1)


def cycle(fine, second, deep, strips, corr_ref, res_ref, *spread):
    place = tuple(lax.axis_index(a) for a in AXES)
    count = tuple(lax.axis_size(a) for a in AXES)
    solved, sources, centres, seen = [], [], [], {}
    for level in range(4):
        d, rows, cols, tall = DEPTH[level], ROWS[level], COLS[level], TALL[level]
        lane, row = iota((tall, LANES), 1), iota((tall, LANES), 0)
        y = row - 8
        y_all = place[1] * rows + y
        y_ok = (y >= -HALO) & (y < rows + HALO) & (y_all >= 0) & (y_all < count[1] * rows)
        near = lane < cols
        right = (lane >= cols % LANES) & (lane < cols % LANES + HALO)
        leftward = lane >= LANES - HALO
        side_ok = (right & (place[2] < count[2] - 1)) | (leftward & (place[2] > 0))
        oks = [y_ok, y_ok & side_ok] if level == 0 else [y_ok & (near | side_ok)]
        src, cen, inv = [], [], []
        for z in range(-HALO, d + HALO):
            z_all = place[0] * d + z
            z_ok = (z_all >= 0) & (z_all < count[0] * d)
            both = []
            for a in range(2):
                main = own(fine, second, deep, level, a, z, seen)
                sides = put(leftward, columns(strips, level, a, z, 0, LANES - HALO, seen), columns(strips, level, a, z, 1, cols % LANES, seen))
                both.append([main, sides] if level == 0 else [put(near, main, sides)])
            oks_z = [ok & z_ok for ok in oks]
            src.append([put(ok, v, 0.0) for ok, v in zip(oks_z, both[0])])
            coef = [put(ok, v, 0.0) for ok, v in zip(oks_z, both[1])]
            cen.append([v + 16.0 for v in coef])
            inv.append([put(ok, 1.0 / (v + 14.0), 0.0) for ok, v in zip(oks_z, coef)])
        planes = [[TAUS[0] * s * i for s, i in zip(sz, iz)] for sz, iz in zip(src, inv)]
        for k in (1, 2):
            new = [None] * len(planes)
            for z in range(k, len(planes) - k):
                around = triple(planes, z)
                new[z] = [x + TAUS[k] * (s - m * x + 0.25 * t) * i for x, s, m, t, i in zip(planes[z], src[z], cen[z], around, inv[z])]
            planes = new
        solved.append(planes)
        sources.append(src)
        centres.append(cen)

    total = solved[3]
    for level in (2, 1, 0):
        tall = TALL[level]
        width = 2 * LANES if level == 0 else LANES
        col = iota((LANES, width), 1)
        col = put(col >= width - width // 4, col - width, col)
        pick = jnp.where(((col >> 1) & (LANES - 1)) == iota((LANES, width), 0), 1.0, 0.0)
        buf, wide = spread[2 * level], spread[2 * level + 1]
        coarse = DEPTH[level + 1]
        for n in range(coarse + 2):
            buf[n] = total[n + 2][0]
        for n in range(coarse + 2):
            half = buf[n, 4 : 4 + tall // 2, :]
            half = jnp.dot(half, pick, precision=EXACT, preferred_element_type=jnp.float32)
            for dy in range(2):
                for k in range(width // LANES):
                    wide[n, k, pl.ds(dy, tall // 2, stride=2), :] = half[:, k * LANES : (k + 1) * LANES]
        new = [None] * len(solved[level])
        share = 0.5 if level == 0 else 1.0
        for z in range(-1, DEPTH[level] + 1):
            n = (z >> 1) + 1
            new[z + 3] = [x + share * wide[n, k] for k, x in enumerate(solved[level][z + 3])]
        total = new
    for z in range(8):
        corr_ref[z] = total[z + 3][0][8:40]
        around = triple(total, z + 3)[0]
        res = sources[0][z + 3][0] - centres[0][z + 3][0] * total[z + 3][0] + 0.25 * around
        res_ref[z] = res[8:40]


def per_device(right_side, reaction):
    f32 = jnp.float32
    vmem = pl.BlockSpec(memory_space=pltpu.VMEM)
    shapes = [(2, 14, 48, LANES), (10, 32, LANES), (7, 3, 16, LANES), (7, 3, 2, 24, LANES)]
    dma = pltpu.SemaphoreType.DMA
    blocks = 3 * len(NEAR) + len(FAR)
    extended = pl.pallas_call(
        exchange,
        out_shape=[jax.ShapeDtypeStruct(shape, f32) for shape in shapes],
        in_specs=[pl.BlockSpec(memory_space=pltpu.HBM)] * 2,
        out_specs=[vmem] * 4,
        scratch_shapes=[
            pltpu.VMEM((2, 4, 16, LANES), f32),
            pltpu.VMEM((2, 2, 8, LANES), f32),
            pltpu.VMEM((2, 8, LANES), f32),
            pltpu.VMEM((2, 24, LANES), f32),
            dma((2,)),
            dma((2,)),
            dma((2,)),
            dma((blocks,)),
            dma((blocks,)),
            dma((20,)),
            dma((20,)),
        ],
        compiler_params=pltpu.CompilerParams(collective_id=0, has_side_effects=True, vmem_limit_bytes=16 * 1024 * 1024),
    )(right_side, reaction)
    block = jax.ShapeDtypeStruct(right_side.shape, f32)
    spread = []
    for level in (0, 1, 2):
        n = DEPTH[level + 1] + 2
        spread.append(pltpu.VMEM((n, TALL[level + 1], LANES), f32))
        spread.append(pltpu.VMEM((n, 2 if level == 0 else 1, TALL[level], LANES), f32))
    return pl.pallas_call(
        cycle,
        out_shape=[block, block],
        in_specs=[vmem] * 4,
        out_specs=[vmem] * 2,
        scratch_shapes=spread,
        compiler_params=pltpu.CompilerParams(vmem_limit_bytes=16 * 1024 * 1024),
    )(*extended)


def solution(mesh):
    spec = P(*AXES)
    return jax.shard_map(
        lambda s, c: tuple(per_device(s, c)),
        mesh=mesh,
        in_specs=(spec, spec),
        out_specs=(spec, spec),
        check_vma=False,
    )
```

```python
import functools
import math

import jax
import jax.numpy as jnp
from jax import lax
from jax.experimental import pallas as pl
from jax.experimental.pallas import tpu as pltpu
from jax.sharding import PartitionSpec as P

MESH = pl.DeviceIdType.MESH
AXES = ("grp", "gy", "gx")
TAUS = tuple(1.0 / (1.15 + 0.85 * math.cos((2 * k - 1) * math.pi / 6.0)) for k in (1, 2, 3))
LANES = 128
HALO = 3
DEPTH = (8, 4, 2, 1)
ROWS = (32, 16, 8, 4)
COLS = (128, 64, 32, 16)
TALL = (48, 32, 24, 16)
NEAR = tuple((dz, dy) for dz in (-1, 0, 1) for dy in (-1, 0, 1) if dz or dy)
FAR = tuple((dz, dy) for dz in (-3, 3, -2, 2) for dy in (-1, 0, 1))


def iota(shape, dim):
    return lax.broadcasted_iota(jnp.int32, shape, dim)


def put(cond, value, other):
    return jnp.where(cond, value, other)


def exact_dot(rows, pick):
    high = rows.astype(jnp.bfloat16)
    rest = rows - high.astype(jnp.float32)
    middle = rest.astype(jnp.bfloat16)
    low = (rest - middle.astype(jnp.float32)).astype(jnp.bfloat16)
    terms = jnp.concatenate([high, middle, low], axis=0)
    out = jnp.dot(terms, pick.astype(jnp.bfloat16), preferred_element_type=jnp.float32)
    n = rows.shape[0]
    return out[:n] + out[n : 2 * n] + out[2 * n :]


def slide(cells, width):
    row = iota(cells.shape, 0)
    for k in (1, 2, 4):
        cells = put(row & k != 0, pltpu.roll(cells, k * width % LANES, 1), cells)
    return cells


def in_row(cells, width):
    return jnp.sum(slide(cells, width), axis=0, keepdims=True)


def off_row(row, width):
    return slide(jnp.broadcast_to(row, (8, LANES)), LANES - width)


def exchange(both, fine, second, deep, strips, sums2, sums3, sums4, msg, xs, xr, bs, br, fs, fr):
    place = tuple(lax.axis_index(a) for a in AXES)
    count = tuple(lax.axis_size(a) for a in AXES)

    def exists(*steps):
        ok = True
        for p, n, step in zip(place, count, steps):
            if step > 0:
                ok = ok & (p < n - step)
            if step < 0:
                ok = ok & (p >= -step)
        return ok

    def device(*steps):
        return tuple(p + step for p, step in zip(place, steps))

    peers = [(0, 0, -1), (0, 0, 1)] + [(dz, dy, 0) for dz, dy in FAR + NEAR]
    barrier = pltpu.get_barrier_semaphore()
    for peer in peers:

        @pl.when(exists(*peer))
        def _():
            pl.semaphore_signal(barrier, inc=1, device_id=device(*peer), device_id_type=MESH)

    fine[:, 3:11, 8:40, :] = both[...]

    for a in range(2):
        for k in range(4):
            sums2[a, k] = sum(fine[a, 3 + 2 * k + dz, pl.ds(8 + dy, 16, stride=2), :] for dz in range(2) for dy in range(2))
        for k in range(2):
            sums3[a, k] = sum(sums2[a, 2 * k + dz, pl.ds(dy, 8, stride=2), :] for dz in range(2) for dy in range(2))
        last = sum(sums3[a, dz, pl.ds(dy, 4, stride=2), :] for dz in range(2) for dy in range(2))
        sums4[a, 0:4] = last
        sums4[a, 4:8] = jnp.zeros_like(last)

    def mean(level, rows):
        pick = jnp.where((iota((LANES, LANES), 0) >> level) == iota((LANES, LANES), 1), 0.125**level, 0.0)
        return exact_dot(rows, pick)

    level2 = mean(1, sums2[...].reshape(128, LANES))
    second[3:7, 8:24, :] = (level2[:64] + pltpu.roll(level2[64:], 64, 1)).reshape(4, 16, LANES)
    level3 = mean(2, sums3[...].reshape(32, LANES))
    level3 = sum(pltpu.roll(level3[16 * a + 8 * z : 16 * a + 8 * z + 8], 64 * z + 32 * a, 1) for a in range(2) for z in range(2))
    level4 = mean(3, sums4[...].reshape(16, LANES))
    level4 = in_row(level4[:8] + pltpu.roll(level4[8:], 16, 1), 32)
    deep[3, 1, 0:8] = level3
    deep[3, 1, 8:9] = level4

    def gather(parts, rows):
        lane = iota((rows, LANES), 1)
        packs = [jnp.zeros((rows, LANES), jnp.float32)] * 2
        for cells, at, first, cols in parts:
            here = (lane >= at) & (lane < at + HALO)
            packs[0] = put(here, pltpu.roll(cells, (at - first) % LANES, 1), packs[0])
            packs[1] = put(here, pltpu.roll(cells, (at - first - cols + HALO) % LANES, 1), packs[1])
        return packs

    parts = []
    for a in range(2):
        for z in range(8):
            for half in range(2):
                cells = fine[a, 3 + z, 8 + 16 * half : 24 + 16 * half]
                parts.append((cells, 48 * half + 6 * z + 3 * a, 0, 128))
        for z in range(4):
            parts.append((second[3 + z, 8:24], 96 + 6 * z + 3 * a, 64 * a, 64))
    upper = gather(parts, 16)
    parts = []
    for a in range(2):
        for z in range(2):
            parts.append((level3, 6 * z + 3 * a, 64 * z + 32 * a, 32))
    lower = gather(parts, 8)
    last = off_row(level4, 32)
    last = gather([(last, 3 * a, 16 * a, 16) for a in range(2)], 8)
    for side in range(2):
        msg[side, 0:8] = upper[side][8:16]
        msg[side, 8:9] = in_row(lower[side], 16)
        msg[side, 9:10] = in_row(last[side], 16)
        msg[side, 10:18] = upper[side][0:8]

    expected = 0
    for peer in peers:
        expected = expected + jnp.where(exists(*peer), 1, 0)
    pl.semaphore_wait(barrier, expected)

    def remote(src, dst, sems, n, *peer):
        copy = pltpu.make_async_remote_copy(
            src_ref=src, dst_ref=dst, send_sem=sems[0].at[n], recv_sem=sems[1].at[n], device_id=device(*peer), device_id_type=MESH
        )
        pl.when(exists(*peer))(copy.start)
        return copy, exists(*peer), exists(*(-step for step in peer))

    def landed(copies):
        for copy, _, fro in copies:
            pl.when(fro)(copy.wait_recv)

    across = [remote(msg.at[side, 0:18], strips.at[3, 1, 1 - side, 0:18], (xs, xr), side, 0, 0, 2 * side - 1) for side in range(2)]

    blocks = []
    for dz, dy in NEAR + FAR:
        for ref, depth, rows in ((fine, 8, 32), (second, 4, 16)):
            if abs(dz) > 1:
                continue
            z0, z1 = {-1: (3, 6), 0: (3, 3 + depth), 1: (depth, 3 + depth)}[dz]
            y0, y1 = {-1: (8, 11), 0: (8, 8 + rows), 1: (rows + 5, rows + 8)}[dy]
            up, along = z0 - dz * depth, y0 - dy * rows
            src, dst = ref, ref
            if ref is fine:
                src, dst = fine.at[:, z0:z1, y0:y1, :], fine.at[:, up : up + z1 - z0, along : along + y1 - y0, :]
            else:
                src, dst = second.at[z0:z1, y0:y1, :], second.at[up : up + z1 - z0, along : along + y1 - y0, :]
            blocks.append(remote(src, dst, (bs, br), len(blocks), dz, dy, 0))
        rows = slice(8, 9) if abs(dz) == 3 else slice(0, 9)
        blocks.append(remote(deep.at[3, 1, rows], deep.at[3 - dz, 1 - dy, rows], (bs, br), len(blocks), dz, dy, 0))

    landed(across)
    passed = []
    for dz, dy in FAR + NEAR:
        rows = slice(8, 10) if abs(dz) > 1 else {-1: slice(8, 13), 0: slice(0, 18), 1: slice(5, 10)}[dy]
        passed.append(remote(strips.at[3, 1, :, rows, :], strips.at[3 - dz, 1 - dy, :, rows, :], (fs, fr), len(passed), dz, dy, 0))
    landed(blocks + passed)
    for copy, to, _ in across + blocks + passed:
        pl.when(to)(copy.wait_send)


def ring_roll(chunks, shift):
    turned = [pltpu.roll(c, shift % LANES, 1) for c in chunks]
    if len(chunks) == 1:
        return turned
    lane = iota(chunks[0].shape, 1)
    edge = lane == (0 if shift > 0 else LANES - 1)
    return [put(edge, turned[1 - k], turned[k]) for k in range(2)]


def triple(planes, z):
    out = []
    for k in range(len(planes[z])):
        v = planes[z - 1][k] + 2.0 * planes[z][k] + planes[z + 1][k]
        n = v.shape[0]
        out.append(pltpu.roll(v, 1, 0) + 2.0 * v + pltpu.roll(v, n - 1, 0))
    before, after = ring_roll(out, 1), ring_roll(out, -1)
    return [b + 2.0 * v + f for b, v, f in zip(before, out, after)]


def columns(strips, level, a, z, side, first, seen):
    dz, p = z // DEPTH[level], z % DEPTH[level]

    def tiles(dy, lane, *which):
        rows = [strips[dz + 3, dy + 1, side, 10:18] if t == 0 else strips[dz + 3, dy + 1, side, 0:8] for t in which]
        rows = rows[0] if len(rows) == 1 else jnp.concatenate(rows, axis=0)
        return pltpu.roll(rows, (first - lane) % LANES, 1)

    if level == 0:
        low, high = 6 * p + 3 * a, 48 + 6 * p + 3 * a
        pieces = [tiles(-1, high, 1), tiles(0, low, 0, 1), tiles(0, high, 0, 1), tiles(1, low, 0)]
    elif level == 1:
        at = 96 + 6 * p + 3 * a
        pieces = [tiles(-1, at, 1), tiles(0, at, 0, 1), tiles(1, at, 0)]
    else:
        pieces = []
        for dy in range(3):
            key = (level, dz, dy, side)
            if key not in seen:
                seen[key] = off_row(strips[dz + 3, dy, side, level + 6 : level + 7], 16)
            cells = seen[key]
            pieces.append(pltpu.roll(cells, (first - 6 * p - 3 * a) % LANES, 1))
        if level == 3:
            pieces = [pieces[0], put(iota((8, LANES), 0) < 4, pieces[1], pieces[2])]
    return jnp.concatenate(pieces, axis=0)


def own(fine, second, deep, level, a, z, seen):
    if level == 0:
        return fine[a, z + 3]
    if level == 1:
        return pltpu.roll(second[z + 3], 64, 1) if a else second[z + 3]
    dz, p = z // DEPTH[level], z % DEPTH[level]
    if level == 2:
        return pltpu.roll(jnp.concatenate([deep[dz + 3, dy, 0:8] for dy in range(3)], axis=0), (-64 * p - 32 * a) % LANES, 1)
    if z not in seen:
        seen[z] = [off_row(deep[dz + 3, dy, 8:9], 32) for dy in range(3)]
    pieces = seen[z]
    pieces = [pieces[0], put(iota((8, LANES), 0) < 4, pieces[1], pieces[2])]
    return pltpu.roll(jnp.concatenate(pieces, axis=0), (-16 * a) % LANES, 1)


def cycle(fine, second, deep, strips, corr_ref, res_ref, *spread):
    place = tuple(lax.axis_index(a) for a in AXES)
    count = tuple(lax.axis_size(a) for a in AXES)
    solved, sources, centres, seen = [], [], [], {}
    for level in range(4):
        d, rows, cols, tall = DEPTH[level], ROWS[level], COLS[level], TALL[level]
        lane, row = iota((tall, LANES), 1), iota((tall, LANES), 0)
        y = row - 8
        y_all = place[1] * rows + y
        y_ok = (y >= -HALO) & (y < rows + HALO) & (y_all >= 0) & (y_all < count[1] * rows)
        near = lane < cols
        right = (lane >= cols % LANES) & (lane < cols % LANES + HALO)
        leftward = lane >= LANES - HALO
        side_ok = (right & (place[2] < count[2] - 1)) | (leftward & (place[2] > 0))
        oks = [y_ok, y_ok & side_ok] if level == 0 else [y_ok & (near | side_ok)]
        src, cen, inv = [], [], []
        for z in range(-HALO, d + HALO):
            z_all = place[0] * d + z
            z_ok = (z_all >= 0) & (z_all < count[0] * d)
            both = []
            for a in range(2):
                main = own(fine, second, deep, level, a, z, seen)
                sides = put(leftward, columns(strips, level, a, z, 0, LANES - HALO, seen), columns(strips, level, a, z, 1, cols % LANES, seen))
                both.append([main, sides] if level == 0 else [put(near, main, sides)])
            oks_z = [ok & z_ok for ok in oks]
            src.append([put(ok, v, 0.0) for ok, v in zip(oks_z, both[0])])
            coef = [put(ok, v, 0.0) for ok, v in zip(oks_z, both[1])]
            cen.append([v + 16.0 for v in coef])
            inv.append([put(ok, 1.0 / (v + 14.0), 0.0) for ok, v in zip(oks_z, coef)])
        planes = [[TAUS[0] * s * i for s, i in zip(sz, iz)] for sz, iz in zip(src, inv)]
        for k in (1, 2):
            new = [None] * len(planes)
            for z in range(k, len(planes) - k):
                around = triple(planes, z)
                new[z] = [x + TAUS[k] * (s - m * x + 0.25 * t) * i for x, s, m, t, i in zip(planes[z], src[z], cen[z], around, inv[z])]
            planes = new
        solved.append(planes)
        sources.append(src)
        centres.append(cen)

    total = solved[3]
    for level in (2, 1, 0):
        tall = TALL[level]
        width = 2 * LANES if level == 0 else LANES
        col = iota((LANES, width), 1)
        col = put(col >= width - width // 4, col - width, col)
        pick = jnp.where(((col >> 1) & (LANES - 1)) == iota((LANES, width), 0), 1.0, 0.0)
        buf, wide = spread[2 * level], spread[2 * level + 1]
        coarse = DEPTH[level + 1]
        for n in range(coarse + 2):
            buf[n] = total[n + 2][0]
        halves = exact_dot(jnp.concatenate([buf[n, 4 : 4 + tall // 2, :] for n in range(coarse + 2)], axis=0), pick)
        for n in range(coarse + 2):
            half = halves[n * (tall // 2) : (n + 1) * (tall // 2)]
            for dy in range(2):
                for k in range(width // LANES):
                    wide[n, k, pl.ds(dy, tall // 2, stride=2), :] = half[:, k * LANES : (k + 1) * LANES]
        new = [None] * len(solved[level])
        share = 0.5 if level == 0 else 1.0
        for z in range(-1, DEPTH[level] + 1):
            n = (z >> 1) + 1
            new[z + 3] = [x + share * wide[n, k] for k, x in enumerate(solved[level][z + 3])]
        total = new
    for z in range(8):
        corr_ref[z] = total[z + 3][0][8:40]
        around = triple(total, z + 3)[0]
        res = sources[0][z + 3][0] - centres[0][z + 3][0] * total[z + 3][0] + 0.25 * around
        res_ref[z] = res[8:40]


def per_device(right_side, reaction):
    f32 = jnp.float32
    vmem = pl.BlockSpec(memory_space=pltpu.VMEM)
    shapes = [(2, 14, 48, LANES), (10, 32, LANES), (7, 3, 16, LANES), (7, 3, 2, 24, LANES)]
    dma = pltpu.SemaphoreType.DMA
    blocks = 3 * len(NEAR) + len(FAR)
    extended = pl.pallas_call(
        exchange,
        out_shape=[jax.ShapeDtypeStruct(shape, f32) for shape in shapes],
        in_specs=[vmem],
        out_specs=[vmem] * 4,
        scratch_shapes=[
            pltpu.VMEM((2, 4, 16, LANES), f32),
            pltpu.VMEM((2, 2, 8, LANES), f32),
            pltpu.VMEM((2, 8, LANES), f32),
            pltpu.VMEM((2, 24, LANES), f32),
            dma((2,)),
            dma((2,)),
            dma((blocks,)),
            dma((blocks,)),
            dma((20,)),
            dma((20,)),
        ],
        compiler_params=pltpu.CompilerParams(collective_id=0, has_side_effects=True, vmem_limit_bytes=16 * 1024 * 1024),
    )(jnp.stack([right_side, reaction]))
    block = jax.ShapeDtypeStruct(right_side.shape, f32)
    spread = []
    for level in (0, 1, 2):
        n = DEPTH[level + 1] + 2
        spread.append(pltpu.VMEM((n, TALL[level + 1], LANES), f32))
        spread.append(pltpu.VMEM((n, 2 if level == 0 else 1, TALL[level], LANES), f32))
    return pl.pallas_call(
        cycle,
        out_shape=[block, block],
        in_specs=[vmem] * 4,
        out_specs=[vmem] * 2,
        scratch_shapes=spread,
        compiler_params=pltpu.CompilerParams(vmem_limit_bytes=16 * 1024 * 1024),
    )(*extended)


def solution(mesh):
    spec = P(*AXES)
    return jax.shard_map(
        lambda s, c: tuple(per_device(s, c)),
        mesh=mesh,
        in_specs=(spec, spec),
        out_specs=(spec, spec),
        check_vma=False,
    )
```

```python
import functools
import math

import jax
import jax.numpy as jnp
from jax import lax
from jax.experimental import pallas as pl
from jax.experimental.pallas import tpu as pltpu
from jax.sharding import PartitionSpec as P

MESH = pl.DeviceIdType.MESH
AXES = ("grp", "gy", "gx")
TAUS = tuple(1.0 / (1.15 + 0.85 * math.cos((2 * k - 1) * math.pi / 6.0)) for k in (1, 2, 3))
LANES = 128
HALO = 3
DEPTH = (8, 4, 2, 1)
ROWS = (32, 16, 8, 4)
COLS = (128, 64, 32, 16)
TALL = (48, 32, 24, 16)
NEAR = tuple((dz, dy) for dz in (-1, 0, 1) for dy in (-1, 0, 1) if dz or dy)
FAR = tuple((dz, dy) for dz in (-3, 3, -2, 2) for dy in (-1, 0, 1))


def iota(shape, dim):
    return lax.broadcasted_iota(jnp.int32, shape, dim)


def put(cond, value, other):
    return jnp.where(cond, value, other)


def exact_dot(rows, pick):
    high = rows.astype(jnp.bfloat16)
    rest = rows - high.astype(jnp.float32)
    middle = rest.astype(jnp.bfloat16)
    low = (rest - middle.astype(jnp.float32)).astype(jnp.bfloat16)
    terms = jnp.concatenate([high, middle, low], axis=0)
    out = jnp.dot(terms, pick.astype(jnp.bfloat16), preferred_element_type=jnp.float32)
    n = rows.shape[0]
    return out[:n] + out[n : 2 * n] + out[2 * n :]


def slide(cells, width):
    row = iota(cells.shape, 0)
    for k in (1, 2, 4):
        cells = put(row & k != 0, pltpu.roll(cells, k * width % LANES, 1), cells)
    return cells


def in_row(cells, width):
    return jnp.sum(slide(cells, width), axis=0, keepdims=True)


def off_row(row, width):
    return slide(jnp.broadcast_to(row, (8, LANES)), LANES - width)


def exchange(both, fine, second, deep, strips, sums2, sums3, sums4, msg, xs, xr, bs, br, fs, fr):
    place = tuple(lax.axis_index(a) for a in AXES)
    count = tuple(lax.axis_size(a) for a in AXES)

    def exists(*steps):
        ok = True
        for p, n, step in zip(place, count, steps):
            if step > 0:
                ok = ok & (p < n - step)
            if step < 0:
                ok = ok & (p >= -step)
        return ok

    def device(*steps):
        return tuple(p + step for p, step in zip(place, steps))

    peers = [(0, 0, -1), (0, 0, 1)] + [(dz, dy, 0) for dz, dy in FAR + NEAR]
    barrier = pltpu.get_barrier_semaphore()
    for peer in peers:

        @pl.when(exists(*peer))
        def _():
            pl.semaphore_signal(barrier, inc=1, device_id=device(*peer), device_id_type=MESH)

    fine[:, 3:11, 8:40, :] = both[...]

    for a in range(2):
        for k in range(4):
            sums2[a, k] = sum(fine[a, 3 + 2 * k + dz, pl.ds(8 + dy, 16, stride=2), :] for dz in range(2) for dy in range(2))
        for k in range(2):
            sums3[a, k] = sum(sums2[a, 2 * k + dz, pl.ds(dy, 8, stride=2), :] for dz in range(2) for dy in range(2))
        last = sum(sums3[a, dz, pl.ds(dy, 4, stride=2), :] for dz in range(2) for dy in range(2))
        sums4[a, 0:4] = last
        sums4[a, 4:8] = jnp.zeros_like(last)

    def mean(level, rows):
        pick = jnp.where((iota((LANES, LANES), 0) >> level) == iota((LANES, LANES), 1), 0.125**level, 0.0)
        return exact_dot(rows, pick)

    level2 = mean(1, sums2[...].reshape(128, LANES))
    second[3:7, 8:24, :] = (level2[:64] + pltpu.roll(level2[64:], 64, 1)).reshape(4, 16, LANES)
    level3 = mean(2, sums3[...].reshape(32, LANES))
    level3 = sum(pltpu.roll(level3[16 * a + 8 * z : 16 * a + 8 * z + 8], 64 * z + 32 * a, 1) for a in range(2) for z in range(2))
    level4 = mean(3, sums4[...].reshape(16, LANES))
    level4 = in_row(level4[:8] + pltpu.roll(level4[8:], 16, 1), 32)
    deep[3, 1, 0:8] = level3
    deep[3, 1, 8:9] = level4

    def gather(parts, rows):
        lane = iota((rows, LANES), 1)
        packs = [jnp.zeros((rows, LANES), jnp.float32)] * 2
        for cells, at, first, cols in parts:
            here = (lane >= at) & (lane < at + HALO)
            packs[0] = put(here, pltpu.roll(cells, (at - first) % LANES, 1), packs[0])
            packs[1] = put(here, pltpu.roll(cells, (at - first - cols + HALO) % LANES, 1), packs[1])
        return packs

    parts = []
    for a in range(2):
        for z in range(8):
            for half in range(2):
                cells = fine[a, 3 + z, 8 + 16 * half : 24 + 16 * half]
                parts.append((cells, 48 * half + 6 * z + 3 * a, 0, 128))
        for z in range(4):
            parts.append((second[3 + z, 8:24], 96 + 6 * z + 3 * a, 64 * a, 64))
    upper = gather(parts, 16)
    parts = []
    for a in range(2):
        for z in range(2):
            parts.append((level3, 6 * z + 3 * a, 64 * z + 32 * a, 32))
    lower = gather(parts, 8)
    last = off_row(level4, 32)
    last = gather([(last, 3 * a, 16 * a, 16) for a in range(2)], 8)
    for side in range(2):
        msg[side, 0:8] = upper[side][8:16]
        msg[side, 8:9] = in_row(lower[side], 16)
        msg[side, 9:10] = in_row(last[side], 16)
        msg[side, 10:18] = upper[side][0:8]

    expected = 0
    for peer in peers:
        expected = expected + jnp.where(exists(*peer), 1, 0)
    pl.semaphore_wait(barrier, expected)

    def remote(src, dst, sems, n, *peer):
        return pltpu.make_async_remote_copy(
            src_ref=src, dst_ref=dst, send_sem=sems[0].at[n], recv_sem=sems[1].at[n], device_id=device(*peer), device_id_type=MESH
        )

    def each(copies, do, *peer):
        @pl.when(exists(*peer))
        def _():
            for copy in copies:
                getattr(copy, do)()

    across = {}
    for side, dx in enumerate((-1, 1)):
        across[dx] = [remote(msg.at[side, 0:18], strips.at[3, 1, 1 - side, 0:18], (xs, xr), side, 0, 0, dx)]
        each(across[dx], "start", 0, 0, dx)

    blocks, n = {}, 0
    for dz, dy in NEAR:
        refs = [(deep.at[3, 1, 0:9], deep.at[3 - dz, 1 - dy, 0:9])]
        for ref, depth, rows in ((fine, 8, 32), (second, 4, 16)):
            z0, z1 = {-1: (3, 6), 0: (3, 3 + depth), 1: (depth, 3 + depth)}[dz]
            y0, y1 = {-1: (8, 11), 0: (8, 8 + rows), 1: (rows + 5, rows + 8)}[dy]
            up, along = z0 - dz * depth, y0 - dy * rows
            if ref is fine:
                refs.append((fine.at[:, z0:z1, y0:y1, :], fine.at[:, up : up + z1 - z0, along : along + y1 - y0, :]))
            else:
                refs.append((second.at[z0:z1, y0:y1, :], second.at[up : up + z1 - z0, along : along + y1 - y0, :]))
        blocks[dz, dy] = [remote(src, dst, (bs, br), n + k, dz, dy, 0) for k, (src, dst) in enumerate(refs)]
        n += len(refs)
        each(blocks[dz, dy], "start", dz, dy, 0)

    for dx in (-1, 1):
        each(across[dx], "wait_recv", 0, 0, -dx)
    for side in range(2):
        deep[3, 1, 9 + 2 * side : 11 + 2 * side] = strips[3, 1, side, 8:10]
    passed = {}
    for dz, dy in FAR + NEAR:
        if abs(dz) > 1:
            rows = slice(8, 13) if abs(dz) == 3 else slice(0, 13)
            src, dst = deep.at[3, 1, rows], deep.at[3 - dz, 1 - dy, rows]
        else:
            rows = {-1: slice(8, 13), 0: slice(0, 18), 1: slice(5, 10)}[dy]
            src, dst = strips.at[3, 1, :, rows, :], strips.at[3 - dz, 1 - dy, :, rows, :]
        passed[dz, dy] = [remote(src, dst, (fs, fr), len(passed), dz, dy, 0)]
        each(passed[dz, dy], "start", dz, dy, 0)
    for dx in (-1, 1):
        each(across[dx], "wait_send", 0, 0, dx)
    for dz, dy in NEAR:
        each(blocks[dz, dy], "wait_send", dz, dy, 0)
    for dz, dy in NEAR:
        each(blocks[dz, dy] + passed[dz, dy], "wait_recv", -dz, -dy, 0)
    for dz, dy in FAR:
        each(passed[dz, dy], "wait_recv", -dz, -dy, 0)
    for dz, dy in NEAR + FAR:
        each(passed[dz, dy], "wait_send", dz, dy, 0)


def ring_roll(chunks, shift):
    turned = [pltpu.roll(c, shift % LANES, 1) for c in chunks]
    if len(chunks) == 1:
        return turned
    lane = iota(chunks[0].shape, 1)
    edge = lane == (0 if shift > 0 else LANES - 1)
    return [put(edge, turned[1 - k], turned[k]) for k in range(2)]


def triple(planes, z):
    out = []
    for k in range(len(planes[z])):
        v = planes[z - 1][k] + 2.0 * planes[z][k] + planes[z + 1][k]
        n = v.shape[0]
        out.append(pltpu.roll(v, 1, 0) + 2.0 * v + pltpu.roll(v, n - 1, 0))
    before, after = ring_roll(out, 1), ring_roll(out, -1)
    return [b + 2.0 * v + f for b, v, f in zip(before, out, after)]


def columns(deep, strips, level, a, z, side, first, seen):
    dz, p = z // DEPTH[level], z % DEPTH[level]

    def tiles(dy, lane, *which):
        rows = [strips[dz + 3, dy + 1, side, 10:18] if t == 0 else strips[dz + 3, dy + 1, side, 0:8] for t in which]
        rows = rows[0] if len(rows) == 1 else jnp.concatenate(rows, axis=0)
        return pltpu.roll(rows, (first - lane) % LANES, 1)

    if level == 0:
        low, high = 6 * p + 3 * a, 48 + 6 * p + 3 * a
        pieces = [tiles(-1, high, 1), tiles(0, low, 0, 1), tiles(0, high, 0, 1), tiles(1, low, 0)]
    elif level == 1:
        at = 96 + 6 * p + 3 * a
        pieces = [tiles(-1, at, 1), tiles(0, at, 0, 1), tiles(1, at, 0)]
    else:
        pieces = []
        for dy in range(3):
            key = (level, dz, dy, side)
            if key not in seen:
                near, far = level + 6, 7 + 2 * side + level
                row = strips[dz + 3, dy, side, near : near + 1] if abs(dz) < 2 else deep[dz + 3, dy, far : far + 1]
                seen[key] = off_row(row, 16)
            cells = seen[key]
            pieces.append(pltpu.roll(cells, (first - 6 * p - 3 * a) % LANES, 1))
        if level == 3:
            pieces = [pieces[0], put(iota((8, LANES), 0) < 4, pieces[1], pieces[2])]
    return jnp.concatenate(pieces, axis=0)


def own(fine, second, deep, level, a, z, seen):
    if level == 0:
        return fine[a, z + 3]
    if level == 1:
        return pltpu.roll(second[z + 3], 64, 1) if a else second[z + 3]
    dz, p = z // DEPTH[level], z % DEPTH[level]
    if level == 2:
        return pltpu.roll(jnp.concatenate([deep[dz + 3, dy, 0:8] for dy in range(3)], axis=0), (-64 * p - 32 * a) % LANES, 1)
    if z not in seen:
        seen[z] = [off_row(deep[dz + 3, dy, 8:9], 32) for dy in range(3)]
    pieces = seen[z]
    pieces = [pieces[0], put(iota((8, LANES), 0) < 4, pieces[1], pieces[2])]
    return pltpu.roll(jnp.concatenate(pieces, axis=0), (-16 * a) % LANES, 1)


def cycle(fine, second, deep, strips, corr_ref, res_ref, *spread):
    place = tuple(lax.axis_index(a) for a in AXES)
    count = tuple(lax.axis_size(a) for a in AXES)
    solved, sources, centres, seen = [], [], [], {}
    for level in range(4):
        d, rows, cols, tall = DEPTH[level], ROWS[level], COLS[level], TALL[level]
        lane, row = iota((tall, LANES), 1), iota((tall, LANES), 0)
        y = row - 8
        y_all = place[1] * rows + y
        y_ok = (y >= -HALO) & (y < rows + HALO) & (y_all >= 0) & (y_all < count[1] * rows)
        near = lane < cols
        right = (lane >= cols % LANES) & (lane < cols % LANES + HALO)
        leftward = lane >= LANES - HALO
        side_ok = (right & (place[2] < count[2] - 1)) | (leftward & (place[2] > 0))
        oks = [y_ok, y_ok & side_ok] if level == 0 else [y_ok & (near | side_ok)]
        src, cen, inv = [], [], []
        for z in range(-HALO, d + HALO):
            z_all = place[0] * d + z
            z_ok = (z_all >= 0) & (z_all < count[0] * d)
            both = []
            for a in range(2):
                main = own(fine, second, deep, level, a, z, seen)
                sides = put(leftward, columns(deep, strips, level, a, z, 0, LANES - HALO, seen), columns(deep, strips, level, a, z, 1, cols % LANES, seen))
                both.append([main, sides] if level == 0 else [put(near, main, sides)])
            oks_z = [ok & z_ok for ok in oks]
            src.append([put(ok, v, 0.0) for ok, v in zip(oks_z, both[0])])
            coef = [put(ok, v, 0.0) for ok, v in zip(oks_z, both[1])]
            cen.append([v + 16.0 for v in coef])
            inv.append([put(ok, 1.0 / (v + 14.0), 0.0) for ok, v in zip(oks_z, coef)])
        planes = [[TAUS[0] * s * i for s, i in zip(sz, iz)] for sz, iz in zip(src, inv)]
        for k in (1, 2):
            new = [None] * len(planes)
            for z in range(k, len(planes) - k):
                around = triple(planes, z)
                new[z] = [x + TAUS[k] * (s - m * x + 0.25 * t) * i for x, s, m, t, i in zip(planes[z], src[z], cen[z], around, inv[z])]
            planes = new
        solved.append(planes)
        sources.append(src)
        centres.append(cen)

    total = solved[3]
    for level in (2, 1, 0):
        tall = TALL[level]
        width = 2 * LANES if level == 0 else LANES
        col = iota((LANES, width), 1)
        col = put(col >= width - width // 4, col - width, col)
        pick = jnp.where(((col >> 1) & (LANES - 1)) == iota((LANES, width), 0), 1.0, 0.0)
        buf, wide = spread[2 * level], spread[2 * level + 1]
        coarse = DEPTH[level + 1]
        for n in range(coarse + 2):
            buf[n] = total[n + 2][0]
        halves = exact_dot(jnp.concatenate([buf[n, 4 : 4 + tall // 2, :] for n in range(coarse + 2)], axis=0), pick)
        for n in range(coarse + 2):
            half = halves[n * (tall // 2) : (n + 1) * (tall // 2)]
            for dy in range(2):
                for k in range(width // LANES):
                    wide[n, k, pl.ds(dy, tall // 2, stride=2), :] = half[:, k * LANES : (k + 1) * LANES]
        new = [None] * len(solved[level])
        share = 0.5 if level == 0 else 1.0
        for z in range(-1, DEPTH[level] + 1):
            n = (z >> 1) + 1
            new[z + 3] = [x + share * wide[n, k] for k, x in enumerate(solved[level][z + 3])]
        total = new
    for z in range(8):
        corr_ref[z] = total[z + 3][0][8:40]
        around = triple(total, z + 3)[0]
        res = sources[0][z + 3][0] - centres[0][z + 3][0] * total[z + 3][0] + 0.25 * around
        res_ref[z] = res[8:40]


def per_device(right_side, reaction):
    f32 = jnp.float32
    vmem = pl.BlockSpec(memory_space=pltpu.VMEM)
    shapes = [(2, 14, 48, LANES), (10, 32, LANES), (7, 3, 16, LANES), (7, 3, 2, 24, LANES)]
    dma = pltpu.SemaphoreType.DMA
    blocks = 3 * len(NEAR)
    extended = pl.pallas_call(
        exchange,
        out_shape=[jax.ShapeDtypeStruct(shape, f32) for shape in shapes],
        in_specs=[vmem],
        out_specs=[vmem] * 4,
        scratch_shapes=[
            pltpu.VMEM((2, 4, 16, LANES), f32),
            pltpu.VMEM((2, 2, 8, LANES), f32),
            pltpu.VMEM((2, 8, LANES), f32),
            pltpu.VMEM((2, 24, LANES), f32),
            dma((2,)),
            dma((2,)),
            dma((blocks,)),
            dma((blocks,)),
            dma((20,)),
            dma((20,)),
        ],
        compiler_params=pltpu.CompilerParams(collective_id=0, has_side_effects=True, vmem_limit_bytes=16 * 1024 * 1024),
    )(jnp.stack([right_side, reaction]))
    block = jax.ShapeDtypeStruct(right_side.shape, f32)
    spread = []
    for level in (0, 1, 2):
        n = DEPTH[level + 1] + 2
        spread.append(pltpu.VMEM((n, TALL[level + 1], LANES), f32))
        spread.append(pltpu.VMEM((n, 2 if level == 0 else 1, TALL[level], LANES), f32))
    return pl.pallas_call(
        cycle,
        out_shape=[block, block],
        in_specs=[vmem] * 4,
        out_specs=[vmem] * 2,
        scratch_shapes=spread,
        compiler_params=pltpu.CompilerParams(vmem_limit_bytes=16 * 1024 * 1024),
    )(*extended)


def solution(mesh):
    spec = P(*AXES)
    return jax.shard_map(
        lambda s, c: tuple(per_device(s, c)),
        mesh=mesh,
        in_specs=(spec, spec),
        out_specs=(spec, spec),
        check_vma=False,
    )
```

```python
import functools
import math

import jax
import jax.numpy as jnp
from jax import lax
from jax.experimental import pallas as pl
from jax.experimental.pallas import tpu as pltpu
from jax.sharding import PartitionSpec as P

MESH = pl.DeviceIdType.MESH
AXES = ("grp", "gy", "gx")
TAUS = tuple(1.0 / (1.15 + 0.85 * math.cos((2 * k - 1) * math.pi / 6.0)) for k in (1, 2, 3))
LANES = 128
HALO = 3
DEPTH = (8, 4, 2, 1)
ROWS = (32, 16, 8, 4)
COLS = (128, 64, 32, 16)
TALL = (48, 32, 24, 16)
NEAR = tuple((dz, dy) for dz in (-1, 0, 1) for dy in (-1, 0, 1) if dz or dy)
FAR = (-3, 3, -2, 2)


def iota(shape, dim):
    return lax.broadcasted_iota(jnp.int32, shape, dim)


def put(cond, value, other):
    return jnp.where(cond, value, other)


def exact_dot(rows, pick):
    high = rows.astype(jnp.bfloat16)
    rest = rows - high.astype(jnp.float32)
    middle = rest.astype(jnp.bfloat16)
    low = (rest - middle.astype(jnp.float32)).astype(jnp.bfloat16)
    terms = jnp.concatenate([high, middle, low], axis=0)
    out = jnp.dot(terms, pick.astype(jnp.bfloat16), preferred_element_type=jnp.float32)
    n = rows.shape[0]
    return out[:n] + out[n : 2 * n] + out[2 * n :]


def slide(cells, width):
    row = iota(cells.shape, 0)
    for k in (1, 2, 4):
        cells = put(row & k != 0, pltpu.roll(cells, k * width % LANES, 1), cells)
    return cells


def in_row(cells, width):
    return jnp.sum(slide(cells, width), axis=0, keepdims=True)


def off_row(row, width):
    return slide(jnp.broadcast_to(row, (8, LANES)), LANES - width)


def exchange(both, fine, second, deep, strips, sums2, sums3, sums4, msg, xs, xr, bs, br, fs, fr):
    place = tuple(lax.axis_index(a) for a in AXES)
    count = tuple(lax.axis_size(a) for a in AXES)

    def exists(*steps):
        ok = True
        for p, n, step in zip(place, count, steps):
            if step > 0:
                ok = ok & (p < n - step)
            if step < 0:
                ok = ok & (p >= -step)
        return ok

    def device(*steps):
        return tuple(p + step for p, step in zip(place, steps))

    peers = [(dz, 0, dx) for dz in (0, *FAR) for dx in (-1, 1)] + [(dz, 0, 0) for dz in FAR] + [(dz, dy, 0) for dz, dy in NEAR]
    barrier = pltpu.get_barrier_semaphore()
    for peer in peers:

        @pl.when(exists(*peer))
        def _():
            pl.semaphore_signal(barrier, inc=1, device_id=device(*peer), device_id_type=MESH)

    fine[:, 3:11, 8:40, :] = both[...]

    for a in range(2):
        for k in range(4):
            sums2[a, k] = sum(fine[a, 3 + 2 * k + dz, pl.ds(8 + dy, 16, stride=2), :] for dz in range(2) for dy in range(2))
        for k in range(2):
            sums3[a, k] = sum(sums2[a, 2 * k + dz, pl.ds(dy, 8, stride=2), :] for dz in range(2) for dy in range(2))
        last = sum(sums3[a, dz, pl.ds(dy, 4, stride=2), :] for dz in range(2) for dy in range(2))
        sums4[a, 0:4] = last
        sums4[a, 4:8] = jnp.zeros_like(last)

    def mean(level, rows):
        pick = jnp.where((iota((LANES, LANES), 0) >> level) == iota((LANES, LANES), 1), 0.125**level, 0.0)
        return exact_dot(rows, pick)

    level2 = mean(1, sums2[...].reshape(128, LANES))
    second[3:7, 8:24, :] = (level2[:64] + pltpu.roll(level2[64:], 64, 1)).reshape(4, 16, LANES)
    level3 = mean(2, sums3[...].reshape(32, LANES))
    level3 = sum(pltpu.roll(level3[16 * a + 8 * z : 16 * a + 8 * z + 8], 64 * z + 32 * a, 1) for a in range(2) for z in range(2))
    level4 = mean(3, sums4[...].reshape(16, LANES))
    level4 = in_row(level4[:8] + pltpu.roll(level4[8:], 16, 1), 32)
    deep[3, 1, 0:8] = level3
    deep[3, 1, 8:9] = level4

    def gather(parts, rows):
        lane = iota((rows, LANES), 1)
        packs = [jnp.zeros((rows, LANES), jnp.float32)] * 2
        for cells, at, first, cols in parts:
            here = (lane >= at) & (lane < at + HALO)
            packs[0] = put(here, pltpu.roll(cells, (at - first) % LANES, 1), packs[0])
            packs[1] = put(here, pltpu.roll(cells, (at - first - cols + HALO) % LANES, 1), packs[1])
        return packs

    parts = []
    for a in range(2):
        for z in range(8):
            for half in range(2):
                cells = fine[a, 3 + z, 8 + 16 * half : 24 + 16 * half]
                parts.append((cells, 48 * half + 6 * z + 3 * a, 0, 128))
        for z in range(4):
            parts.append((second[3 + z, 8:24], 96 + 6 * z + 3 * a, 64 * a, 64))
    upper = gather(parts, 16)
    parts = []
    for a in range(2):
        for z in range(2):
            parts.append((level3, 6 * z + 3 * a, 64 * z + 32 * a, 32))
    lower = gather(parts, 8)
    last = off_row(level4, 32)
    last = gather([(last, 3 * a, 16 * a, 16) for a in range(2)], 8)
    for side in range(2):
        msg[side, 0:8] = upper[side][8:16]
        msg[side, 8:9] = in_row(lower[side], 16)
        msg[side, 9:10] = in_row(last[side], 16)
        msg[side, 10:18] = upper[side][0:8]

    expected = 0
    for peer in peers:
        expected = expected + jnp.where(exists(*peer), 1, 0)
    pl.semaphore_wait(barrier, expected)

    def remote(src, dst, sems, n, *peer):
        return pltpu.make_async_remote_copy(
            src_ref=src, dst_ref=dst, send_sem=sems[0].at[n], recv_sem=sems[1].at[n], device_id=device(*peer), device_id_type=MESH
        )

    def each(copies, do, *peer):
        @pl.when(exists(*peer))
        def _():
            for copy in copies:
                getattr(copy, do)()

    across = {}
    for side, dx in enumerate((-1, 1)):
        across[dx] = [remote(msg.at[side, 0:18], strips.at[3, 1, 1 - side, 0:18], (xs, xr), side, 0, 0, dx)]
        each(across[dx], "start", 0, 0, dx)
    distant, m = {}, 2
    for dz in FAR:
        for side, dx in enumerate((-1, 1)):
            at = 9 + 2 * (1 - side)
            distant[dz, dx] = [remote(msg.at[side, 8:10], deep.at[3 - dz, 1, at : at + 2], (xs, xr), m, dz, 0, dx)]
            each(distant[dz, dx], "start", dz, 0, dx)
            m += 1

    column = {}
    for dz in (-1, 1, *FAR):
        rows = slice(8, 9) if abs(dz) == 3 else slice(0, 9)
        column[dz] = [remote(deep.at[3, 1, rows], deep.at[3 - dz, 1, rows], (bs, br), len(column), dz, 0, 0)]
        each(column[dz], "start", dz, 0, 0)
    blocks, n = {}, len(column)
    for dz, dy in NEAR:
        refs = []
        for ref, depth, rows in ((fine, 8, 32), (second, 4, 16)):
            z0, z1 = {-1: (3, 6), 0: (3, 3 + depth), 1: (depth, 3 + depth)}[dz]
            y0, y1 = {-1: (8, 11), 0: (8, 8 + rows), 1: (rows + 5, rows + 8)}[dy]
            up, along = z0 - dz * depth, y0 - dy * rows
            if ref is fine:
                refs.append((fine.at[:, z0:z1, y0:y1, :], fine.at[:, up : up + z1 - z0, along : along + y1 - y0, :]))
            else:
                refs.append((second.at[z0:z1, y0:y1, :], second.at[up : up + z1 - z0, along : along + y1 - y0, :]))
        blocks[dz, dy] = [remote(src, dst, (bs, br), n + k, dz, dy, 0) for k, (src, dst) in enumerate(refs)]
        n += len(refs)
        each(blocks[dz, dy], "start", dz, dy, 0)

    for dx in (-1, 1):
        each(across[dx], "wait_recv", 0, 0, -dx)
    passed = {}
    for dz, dy in NEAR:
        rows = {-1: slice(8, 13), 0: slice(0, 18), 1: slice(5, 10)}[dy]
        src, dst = strips.at[3, 1, :, rows, :], strips.at[3 - dz, 1 - dy, :, rows, :]
        passed[dz, dy] = [remote(src, dst, (fs, fr), len(passed), dz, dy, 0)]
        each(passed[dz, dy], "start", dz, dy, 0)
    for dz in (-1, 1, *FAR):
        each(column[dz], "wait_recv", -dz, 0, 0)
    for dz, dx in distant:
        each(distant[dz, dx], "wait_recv", -dz, 0, -dx)
    along = {}
    for dy in (-1, 1):
        src, dst = deep.at[:, 1, 0:13, :], deep.at[:, 1 - dy, 0:13, :]
        along[dy] = [remote(src, dst, (fs, fr), len(passed) + len(along), 0, dy, 0)]
        each(along[dy], "start", 0, dy, 0)
    for dx in (-1, 1):
        each(across[dx], "wait_send", 0, 0, dx)
    for dz, dx in distant:
        each(distant[dz, dx], "wait_send", dz, 0, dx)
    for dz in (-1, 1, *FAR):
        each(column[dz], "wait_send", dz, 0, 0)
    for dz, dy in NEAR:
        each(blocks[dz, dy], "wait_send", dz, dy, 0)
    for dz, dy in NEAR:
        each(blocks[dz, dy] + passed[dz, dy], "wait_recv", -dz, -dy, 0)
    for dy in (-1, 1):
        each(along[dy], "wait_recv", 0, -dy, 0)
    for dz, dy in NEAR:
        each(passed[dz, dy], "wait_send", dz, dy, 0)
    for dy in (-1, 1):
        each(along[dy], "wait_send", 0, dy, 0)


def ring_roll(chunks, shift):
    turned = [pltpu.roll(c, shift % LANES, 1) for c in chunks]
    if len(chunks) == 1:
        return turned
    lane = iota(chunks[0].shape, 1)
    edge = lane == (0 if shift > 0 else LANES - 1)
    return [put(edge, turned[1 - k], turned[k]) for k in range(2)]


def triple(planes, z):
    out = []
    for k in range(len(planes[z])):
        v = planes[z - 1][k] + 2.0 * planes[z][k] + planes[z + 1][k]
        n = v.shape[0]
        out.append(pltpu.roll(v, 1, 0) + 2.0 * v + pltpu.roll(v, n - 1, 0))
    before, after = ring_roll(out, 1), ring_roll(out, -1)
    return [b + 2.0 * v + f for b, v, f in zip(before, out, after)]


def columns(deep, strips, level, a, z, side, first, seen):
    dz, p = z // DEPTH[level], z % DEPTH[level]

    def tiles(dy, lane, *which):
        rows = [strips[dz + 3, dy + 1, side, 10:18] if t == 0 else strips[dz + 3, dy + 1, side, 0:8] for t in which]
        rows = rows[0] if len(rows) == 1 else jnp.concatenate(rows, axis=0)
        return pltpu.roll(rows, (first - lane) % LANES, 1)

    if level == 0:
        low, high = 6 * p + 3 * a, 48 + 6 * p + 3 * a
        pieces = [tiles(-1, high, 1), tiles(0, low, 0, 1), tiles(0, high, 0, 1), tiles(1, low, 0)]
    elif level == 1:
        at = 96 + 6 * p + 3 * a
        pieces = [tiles(-1, at, 1), tiles(0, at, 0, 1), tiles(1, at, 0)]
    else:
        pieces = []
        for dy in range(3):
            key = (level, dz, dy, side)
            if key not in seen:
                near, far = level + 6, 7 + 2 * side + level
                row = strips[dz + 3, dy, side, near : near + 1] if abs(dz) < 2 else deep[dz + 3, dy, far : far + 1]
                seen[key] = off_row(row, 16)
            cells = seen[key]
            pieces.append(pltpu.roll(cells, (first - 6 * p - 3 * a) % LANES, 1))
        if level == 3:
            pieces = [pieces[0], put(iota((8, LANES), 0) < 4, pieces[1], pieces[2])]
    return jnp.concatenate(pieces, axis=0)


def own(fine, second, deep, level, a, z, seen):
    if level == 0:
        return fine[a, z + 3]
    if level == 1:
        return pltpu.roll(second[z + 3], 64, 1) if a else second[z + 3]
    dz, p = z // DEPTH[level], z % DEPTH[level]
    if level == 2:
        return pltpu.roll(jnp.concatenate([deep[dz + 3, dy, 0:8] for dy in range(3)], axis=0), (-64 * p - 32 * a) % LANES, 1)
    if z not in seen:
        seen[z] = [off_row(deep[dz + 3, dy, 8:9], 32) for dy in range(3)]
    pieces = seen[z]
    pieces = [pieces[0], put(iota((8, LANES), 0) < 4, pieces[1], pieces[2])]
    return pltpu.roll(jnp.concatenate(pieces, axis=0), (-16 * a) % LANES, 1)


def cycle(fine, second, deep, strips, corr_ref, res_ref, *spread):
    place = tuple(lax.axis_index(a) for a in AXES)
    count = tuple(lax.axis_size(a) for a in AXES)
    solved, sources, centres, seen = [], [], [], {}
    for level in range(4):
        d, rows, cols, tall = DEPTH[level], ROWS[level], COLS[level], TALL[level]
        lane, row = iota((tall, LANES), 1), iota((tall, LANES), 0)
        y = row - 8
        y_all = place[1] * rows + y
        y_ok = (y >= -HALO) & (y < rows + HALO) & (y_all >= 0) & (y_all < count[1] * rows)
        near = lane < cols
        right = (lane >= cols % LANES) & (lane < cols % LANES + HALO)
        leftward = lane >= LANES - HALO
        side_ok = (right & (place[2] < count[2] - 1)) | (leftward & (place[2] > 0))
        oks = [y_ok, y_ok & side_ok] if level == 0 else [y_ok & (near | side_ok)]
        src, cen, inv = [], [], []
        for z in range(-HALO, d + HALO):
            z_all = place[0] * d + z
            z_ok = (z_all >= 0) & (z_all < count[0] * d)
            both = []
            for a in range(2):
                main = own(fine, second, deep, level, a, z, seen)
                sides = put(leftward, columns(deep, strips, level, a, z, 0, LANES - HALO, seen), columns(deep, strips, level, a, z, 1, cols % LANES, seen))
                both.append([main, sides] if level == 0 else [put(near, main, sides)])
            oks_z = [ok & z_ok for ok in oks]
            src.append([put(ok, v, 0.0) for ok, v in zip(oks_z, both[0])])
            coef = [put(ok, v, 0.0) for ok, v in zip(oks_z, both[1])]
            cen.append([v + 16.0 for v in coef])
            inv.append([put(ok, 1.0 / (v + 14.0), 0.0) for ok, v in zip(oks_z, coef)])
        planes = [[TAUS[0] * s * i for s, i in zip(sz, iz)] for sz, iz in zip(src, inv)]
        for k in (1, 2):
            new = [None] * len(planes)
            for z in range(k, len(planes) - k):
                around = triple(planes, z)
                new[z] = [x + TAUS[k] * (s - m * x + 0.25 * t) * i for x, s, m, t, i in zip(planes[z], src[z], cen[z], around, inv[z])]
            planes = new
        solved.append(planes)
        sources.append(src)
        centres.append(cen)

    total = solved[3]
    for level in (2, 1, 0):
        tall = TALL[level]
        width = 2 * LANES if level == 0 else LANES
        col = iota((LANES, width), 1)
        col = put(col >= width - width // 4, col - width, col)
        pick = jnp.where(((col >> 1) & (LANES - 1)) == iota((LANES, width), 0), 1.0, 0.0)
        buf, wide = spread[2 * level], spread[2 * level + 1]
        coarse = DEPTH[level + 1]
        for n in range(coarse + 2):
            buf[n] = total[n + 2][0]
        halves = exact_dot(jnp.concatenate([buf[n, 4 : 4 + tall // 2, :] for n in range(coarse + 2)], axis=0), pick)
        for n in range(coarse + 2):
            half = halves[n * (tall // 2) : (n + 1) * (tall // 2)]
            for dy in range(2):
                for k in range(width // LANES):
                    wide[n, k, pl.ds(dy, tall // 2, stride=2), :] = half[:, k * LANES : (k + 1) * LANES]
        new = [None] * len(solved[level])
        share = 0.5 if level == 0 else 1.0
        for z in range(-1, DEPTH[level] + 1):
            n = (z >> 1) + 1
            new[z + 3] = [x + share * wide[n, k] for k, x in enumerate(solved[level][z + 3])]
        total = new
    for z in range(8):
        corr_ref[z] = total[z + 3][0][8:40]
        around = triple(total, z + 3)[0]
        res = sources[0][z + 3][0] - centres[0][z + 3][0] * total[z + 3][0] + 0.25 * around
        res_ref[z] = res[8:40]


def per_device(right_side, reaction):
    f32 = jnp.float32
    vmem = pl.BlockSpec(memory_space=pltpu.VMEM)
    shapes = [(2, 14, 48, LANES), (10, 32, LANES), (7, 3, 16, LANES), (7, 3, 2, 24, LANES)]
    dma = pltpu.SemaphoreType.DMA
    blocks = 2 * len(NEAR) + 6
    extended = pl.pallas_call(
        exchange,
        out_shape=[jax.ShapeDtypeStruct(shape, f32) for shape in shapes],
        in_specs=[vmem],
        out_specs=[vmem] * 4,
        scratch_shapes=[
            pltpu.VMEM((2, 4, 16, LANES), f32),
            pltpu.VMEM((2, 2, 8, LANES), f32),
            pltpu.VMEM((2, 8, LANES), f32),
            pltpu.VMEM((2, 24, LANES), f32),
            dma((10,)),
            dma((10,)),
            dma((blocks,)),
            dma((blocks,)),
            dma((10,)),
            dma((10,)),
        ],
        compiler_params=pltpu.CompilerParams(collective_id=0, has_side_effects=True, vmem_limit_bytes=16 * 1024 * 1024),
    )(jnp.stack([right_side, reaction]))
    block = jax.ShapeDtypeStruct(right_side.shape, f32)
    spread = []
    for level in (0, 1, 2):
        n = DEPTH[level + 1] + 2
        spread.append(pltpu.VMEM((n, TALL[level + 1], LANES), f32))
        spread.append(pltpu.VMEM((n, 2 if level == 0 else 1, TALL[level], LANES), f32))
    return pl.pallas_call(
        cycle,
        out_shape=[block, block],
        in_specs=[vmem] * 4,
        out_specs=[vmem] * 2,
        scratch_shapes=spread,
        compiler_params=pltpu.CompilerParams(vmem_limit_bytes=16 * 1024 * 1024),
    )(*extended)


def solution(mesh):
    spec = P(*AXES)
    return jax.shard_map(
        lambda s, c: tuple(per_device(s, c)),
        mesh=mesh,
        in_specs=(spec, spec),
        out_specs=(spec, spec),
        check_vma=False,
    )
```

```python
import functools
import math

import jax
import jax.numpy as jnp
from jax import lax
from jax.experimental import pallas as pl
from jax.experimental.pallas import tpu as pltpu
from jax.sharding import PartitionSpec as P

MESH = pl.DeviceIdType.MESH
AXES = ("grp", "gy", "gx")
TAUS = tuple(1.0 / (1.15 + 0.85 * math.cos((2 * k - 1) * math.pi / 6.0)) for k in (1, 2, 3))
LANES = 128
HALO = 3
DEPTH = (8, 4, 2, 1)
ROWS = (32, 16, 8, 4)
COLS = (128, 64, 32, 16)
TALL = (48, 32, 24, 16)
NEAR = ((0, -1), (0, 1), (-1, -1), (-1, 1), (1, -1), (1, 1), (-1, 0), (1, 0))
FAR = (-3, 3, -2, 2)


def iota(shape, dim):
    return lax.broadcasted_iota(jnp.int32, shape, dim)


def put(cond, value, other):
    return jnp.where(cond, value, other)


def exact_dot(rows, pick):
    high = rows.astype(jnp.bfloat16)
    rest = rows - high.astype(jnp.float32)
    middle = rest.astype(jnp.bfloat16)
    low = (rest - middle.astype(jnp.float32)).astype(jnp.bfloat16)
    terms = jnp.concatenate([high, middle, low], axis=0)
    out = jnp.dot(terms, pick.astype(jnp.bfloat16), preferred_element_type=jnp.float32)
    n = rows.shape[0]
    return out[:n] + out[n : 2 * n] + out[2 * n :]


def slide(cells, width):
    row = iota(cells.shape, 0)
    for k in (1, 2, 4):
        cells = put(row & k != 0, pltpu.roll(cells, k * width % LANES, 1), cells)
    return cells


def in_row(cells, width):
    return jnp.sum(slide(cells, width), axis=0, keepdims=True)


def off_row(row, width):
    return slide(jnp.broadcast_to(row, (8, LANES)), LANES - width)


def exchange(both, fine, second, deep, strips, sums2, sums3, sums4, msg, xs, xr, bs, br, fs, fr):
    place = tuple(lax.axis_index(a) for a in AXES)
    count = tuple(lax.axis_size(a) for a in AXES)

    def exists(*steps):
        ok = True
        for p, n, step in zip(place, count, steps):
            if step > 0:
                ok = ok & (p < n - step)
            if step < 0:
                ok = ok & (p >= -step)
        return ok

    def device(*steps):
        return tuple(p + step for p, step in zip(place, steps))

    peers = [(dz, 0, 0) for dz in FAR] + [(0, 0, -1), (0, 0, 1)] + [(dz, dy, 0) for dz, dy in NEAR] + [(dz, 0, dx) for dz in FAR for dx in (-1, 1)]
    barrier = pltpu.get_barrier_semaphore()
    for peer in peers:

        @pl.when(exists(*peer))
        def _():
            pl.semaphore_signal(barrier, inc=1, device_id=device(*peer), device_id_type=MESH)

    fine[:, 3:11, 8:40, :] = both[...]

    for a in range(2):
        for k in range(4):
            sums2[a, k] = sum(fine[a, 3 + 2 * k + dz, pl.ds(8 + dy, 16, stride=2), :] for dz in range(2) for dy in range(2))
        for k in range(2):
            sums3[a, k] = sum(sums2[a, 2 * k + dz, pl.ds(dy, 8, stride=2), :] for dz in range(2) for dy in range(2))
        last = sum(sums3[a, dz, pl.ds(dy, 4, stride=2), :] for dz in range(2) for dy in range(2))
        sums4[a, 0:4] = last
        sums4[a, 4:8] = jnp.zeros_like(last)

    def mean(level, rows):
        pick = jnp.where((iota((LANES, LANES), 0) >> level) == iota((LANES, LANES), 1), 0.125**level, 0.0)
        return exact_dot(rows, pick)

    level2 = mean(1, sums2[...].reshape(128, LANES))
    second[3:7, 8:24, :] = (level2[:64] + pltpu.roll(level2[64:], 64, 1)).reshape(4, 16, LANES)
    level3 = mean(2, sums3[...].reshape(32, LANES))
    level3 = sum(pltpu.roll(level3[16 * a + 8 * z : 16 * a + 8 * z + 8], 64 * z + 32 * a, 1) for a in range(2) for z in range(2))
    level4 = mean(3, sums4[...].reshape(16, LANES))
    level4 = in_row(level4[:8] + pltpu.roll(level4[8:], 16, 1), 32)
    deep[3, 1, 0:8] = level3
    deep[3, 1, 8:9] = level4

    def gather(parts, rows):
        lane = iota((rows, LANES), 1)
        packs = [jnp.zeros((rows, LANES), jnp.float32)] * 2
        for cells, at, first, cols in parts:
            here = (lane >= at) & (lane < at + HALO)
            packs[0] = put(here, pltpu.roll(cells, (at - first) % LANES, 1), packs[0])
            packs[1] = put(here, pltpu.roll(cells, (at - first - cols + HALO) % LANES, 1), packs[1])
        return packs

    parts = []
    for a in range(2):
        for z in range(8):
            for half in range(2):
                cells = fine[a, 3 + z, 8 + 16 * half : 24 + 16 * half]
                parts.append((cells, 48 * half + 6 * z + 3 * a, 0, 128))
        for z in range(4):
            parts.append((second[3 + z, 8:24], 96 + 6 * z + 3 * a, 64 * a, 64))
    upper = gather(parts, 16)
    parts = []
    for a in range(2):
        for z in range(2):
            parts.append((level3, 6 * z + 3 * a, 64 * z + 32 * a, 32))
    lower = gather(parts, 8)
    last = off_row(level4, 32)
    last = gather([(last, 3 * a, 16 * a, 16) for a in range(2)], 8)
    for side in range(2):
        msg[side, 0:8] = upper[side][8:16]
        msg[side, 8:9] = in_row(lower[side], 16)
        msg[side, 9:10] = in_row(last[side], 16)
        msg[side, 10:18] = upper[side][0:8]

    expected = 0
    for peer in peers:
        expected = expected + jnp.where(exists(*peer), 1, 0)
    pl.semaphore_wait(barrier, expected)

    def remote(src, dst, sems, n, *peer):
        return pltpu.make_async_remote_copy(
            src_ref=src, dst_ref=dst, send_sem=sems[0].at[n], recv_sem=sems[1].at[n], device_id=device(*peer), device_id_type=MESH
        )

    def each(copies, do, *peer):
        @pl.when(exists(*peer))
        def _():
            for copy in copies:
                getattr(copy, do)()

    across = {}
    for side, dx in enumerate((-1, 1)):
        across[dx] = [remote(msg.at[side, 0:18], strips.at[3, 1, 1 - side, 0:18], (xs, xr), side, 0, 0, dx)]
        each(across[dx], "start", 0, 0, dx)
    column = {}
    for dz in (-1, 1, *FAR):
        rows = slice(8, 9) if abs(dz) == 3 else slice(0, 9)
        column[dz] = [remote(deep.at[3, 1, rows], deep.at[3 - dz, 1, rows], (bs, br), len(column), dz, 0, 0)]
        each(column[dz], "start", dz, 0, 0)
    distant, m = {}, 2
    for dz in FAR:
        for side, dx in enumerate((-1, 1)):
            at = 9 + 2 * (1 - side)
            distant[dz, dx] = [remote(msg.at[side, 8:10], deep.at[3 - dz, 1, at : at + 2], (xs, xr), m, dz, 0, dx)]
            each(distant[dz, dx], "start", dz, 0, dx)
            m += 1
    blocks, n = {}, len(column)
    for dz, dy in NEAR:
        refs = []
        for ref, depth, rows in ((fine, 8, 32), (second, 4, 16)):
            z0, z1 = {-1: (3, 6), 0: (3, 3 + depth), 1: (depth, 3 + depth)}[dz]
            y0, y1 = {-1: (8, 11), 0: (8, 8 + rows), 1: (rows + 5, rows + 8)}[dy]
            up, along = z0 - dz * depth, y0 - dy * rows
            if ref is fine:
                refs.append((fine.at[:, z0:z1, y0:y1, :], fine.at[:, up : up + z1 - z0, along : along + y1 - y0, :]))
            else:
                refs.append((second.at[z0:z1, y0:y1, :], second.at[up : up + z1 - z0, along : along + y1 - y0, :]))
        blocks[dz, dy] = [remote(src, dst, (bs, br), n + k, dz, dy, 0) for k, (src, dst) in enumerate(refs)]
        n += len(refs)
        each(blocks[dz, dy], "start", dz, dy, 0)

    for dx in (-1, 1):
        each(across[dx], "wait_recv", 0, 0, -dx)
    passed = {}
    for dz, dy in NEAR:
        rows = {-1: slice(8, 13), 0: slice(0, 18), 1: slice(5, 10)}[dy]
        src, dst = strips.at[3, 1, :, rows, :], strips.at[3 - dz, 1 - dy, :, rows, :]
        passed[dz, dy] = [remote(src, dst, (fs, fr), len(passed), dz, dy, 0)]
        each(passed[dz, dy], "start", dz, dy, 0)
    for dz in (-1, 1, *FAR):
        each(column[dz], "wait_recv", -dz, 0, 0)
    for dz, dx in distant:
        each(distant[dz, dx], "wait_recv", -dz, 0, -dx)
    along = {}
    for dy in (-1, 1):
        src, dst = deep.at[:, 1, 0:13, :], deep.at[:, 1 - dy, 0:13, :]
        along[dy] = [remote(src, dst, (fs, fr), len(passed) + len(along), 0, dy, 0)]
        each(along[dy], "start", 0, dy, 0)
    for dx in (-1, 1):
        each(across[dx], "wait_send", 0, 0, dx)
    for dz, dx in distant:
        each(distant[dz, dx], "wait_send", dz, 0, dx)
    for dz in (-1, 1, *FAR):
        each(column[dz], "wait_send", dz, 0, 0)
    for dz, dy in NEAR:
        each(blocks[dz, dy], "wait_send", dz, dy, 0)
    for dz, dy in NEAR:
        each(blocks[dz, dy] + passed[dz, dy], "wait_recv", -dz, -dy, 0)
    for dy in (-1, 1):
        each(along[dy], "wait_recv", 0, -dy, 0)
    for dz, dy in NEAR:
        each(passed[dz, dy], "wait_send", dz, dy, 0)
    for dy in (-1, 1):
        each(along[dy], "wait_send", 0, dy, 0)


def ring_roll(chunks, shift):
    turned = [pltpu.roll(c, shift % LANES, 1) for c in chunks]
    if len(chunks) == 1:
        return turned
    lane = iota(chunks[0].shape, 1)
    edge = lane == (0 if shift > 0 else LANES - 1)
    return [put(edge, turned[1 - k], turned[k]) for k in range(2)]


def triple(planes, z):
    out = []
    for k in range(len(planes[z])):
        v = planes[z - 1][k] + 2.0 * planes[z][k] + planes[z + 1][k]
        n = v.shape[0]
        out.append(pltpu.roll(v, 1, 0) + 2.0 * v + pltpu.roll(v, n - 1, 0))
    before, after = ring_roll(out, 1), ring_roll(out, -1)
    return [b + 2.0 * v + f for b, v, f in zip(before, out, after)]


def columns(deep, strips, level, a, z, side, first, seen):
    dz, p = z // DEPTH[level], z % DEPTH[level]

    def tiles(dy, lane, *which):
        rows = [strips[dz + 3, dy + 1, side, 10:18] if t == 0 else strips[dz + 3, dy + 1, side, 0:8] for t in which]
        rows = rows[0] if len(rows) == 1 else jnp.concatenate(rows, axis=0)
        return pltpu.roll(rows, (first - lane) % LANES, 1)

    if level == 0:
        low, high = 6 * p + 3 * a, 48 + 6 * p + 3 * a
        pieces = [tiles(-1, high, 1), tiles(0, low, 0, 1), tiles(0, high, 0, 1), tiles(1, low, 0)]
    elif level == 1:
        at = 96 + 6 * p + 3 * a
        pieces = [tiles(-1, at, 1), tiles(0, at, 0, 1), tiles(1, at, 0)]
    else:
        pieces = []
        for dy in range(3):
            key = (level, dz, dy, side)
            if key not in seen:
                near, far = level + 6, 7 + 2 * side + level
                row = strips[dz + 3, dy, side, near : near + 1] if abs(dz) < 2 else deep[dz + 3, dy, far : far + 1]
                seen[key] = off_row(row, 16)
            cells = seen[key]
            pieces.append(pltpu.roll(cells, (first - 6 * p - 3 * a) % LANES, 1))
        if level == 3:
            pieces = [pieces[0], put(iota((8, LANES), 0) < 4, pieces[1], pieces[2])]
    return jnp.concatenate(pieces, axis=0)


def own(fine, second, deep, level, a, z, seen):
    if level == 0:
        return fine[a, z + 3]
    if level == 1:
        return pltpu.roll(second[z + 3], 64, 1) if a else second[z + 3]
    dz, p = z // DEPTH[level], z % DEPTH[level]
    if level == 2:
        return pltpu.roll(jnp.concatenate([deep[dz + 3, dy, 0:8] for dy in range(3)], axis=0), (-64 * p - 32 * a) % LANES, 1)
    if z not in seen:
        seen[z] = [off_row(deep[dz + 3, dy, 8:9], 32) for dy in range(3)]
    pieces = seen[z]
    pieces = [pieces[0], put(iota((8, LANES), 0) < 4, pieces[1], pieces[2])]
    return pltpu.roll(jnp.concatenate(pieces, axis=0), (-16 * a) % LANES, 1)


def cycle(fine, second, deep, strips, corr_ref, res_ref, *spread):
    place = tuple(lax.axis_index(a) for a in AXES)
    count = tuple(lax.axis_size(a) for a in AXES)
    solved, sources, centres, seen = [], [], [], {}
    for level in range(4):
        d, rows, cols, tall = DEPTH[level], ROWS[level], COLS[level], TALL[level]
        lane, row = iota((tall, LANES), 1), iota((tall, LANES), 0)
        y = row - 8
        y_all = place[1] * rows + y
        y_ok = (y >= -HALO) & (y < rows + HALO) & (y_all >= 0) & (y_all < count[1] * rows)
        near = lane < cols
        right = (lane >= cols % LANES) & (lane < cols % LANES + HALO)
        leftward = lane >= LANES - HALO
        side_ok = (right & (place[2] < count[2] - 1)) | (leftward & (place[2] > 0))
        oks = [y_ok, y_ok & side_ok] if level == 0 else [y_ok & (near | side_ok)]
        src, cen, inv = [], [], []
        for z in range(-HALO, d + HALO):
            z_all = place[0] * d + z
            z_ok = (z_all >= 0) & (z_all < count[0] * d)
            both = []
            for a in range(2):
                main = own(fine, second, deep, level, a, z, seen)
                sides = put(leftward, columns(deep, strips, level, a, z, 0, LANES - HALO, seen), columns(deep, strips, level, a, z, 1, cols % LANES, seen))
                both.append([main, sides] if level == 0 else [put(near, main, sides)])
            oks_z = [ok & z_ok for ok in oks]
            src.append([put(ok, v, 0.0) for ok, v in zip(oks_z, both[0])])
            coef = [put(ok, v, 0.0) for ok, v in zip(oks_z, both[1])]
            cen.append([v + 16.0 for v in coef])
            inv.append([put(ok, 1.0 / (v + 14.0), 0.0) for ok, v in zip(oks_z, coef)])
        planes = [[TAUS[0] * s * i for s, i in zip(sz, iz)] for sz, iz in zip(src, inv)]
        for k in (1, 2):
            new = [None] * len(planes)
            for z in range(k, len(planes) - k):
                around = triple(planes, z)
                new[z] = [x + TAUS[k] * (s - m * x + 0.25 * t) * i for x, s, m, t, i in zip(planes[z], src[z], cen[z], around, inv[z])]
            planes = new
        solved.append(planes)
        sources.append(src)
        centres.append(cen)

    total = solved[3]
    for level in (2, 1, 0):
        tall = TALL[level]
        width = 2 * LANES if level == 0 else LANES
        col = iota((LANES, width), 1)
        col = put(col >= width - width // 4, col - width, col)
        pick = jnp.where(((col >> 1) & (LANES - 1)) == iota((LANES, width), 0), 1.0, 0.0)
        buf, wide = spread[2 * level], spread[2 * level + 1]
        coarse = DEPTH[level + 1]
        for n in range(coarse + 2):
            buf[n] = total[n + 2][0]
        halves = exact_dot(jnp.concatenate([buf[n, 4 : 4 + tall // 2, :] for n in range(coarse + 2)], axis=0), pick)
        for n in range(coarse + 2):
            half = halves[n * (tall // 2) : (n + 1) * (tall // 2)]
            for dy in range(2):
                for k in range(width // LANES):
                    wide[n, k, pl.ds(dy, tall // 2, stride=2), :] = half[:, k * LANES : (k + 1) * LANES]
        new = [None] * len(solved[level])
        share = 0.5 if level == 0 else 1.0
        for z in range(-1, DEPTH[level] + 1):
            n = (z >> 1) + 1
            new[z + 3] = [x + share * wide[n, k] for k, x in enumerate(solved[level][z + 3])]
        total = new
    for z in range(8):
        corr_ref[z] = total[z + 3][0][8:40]
        around = triple(total, z + 3)[0]
        res = sources[0][z + 3][0] - centres[0][z + 3][0] * total[z + 3][0] + 0.25 * around
        res_ref[z] = res[8:40]


def per_device(right_side, reaction):
    f32 = jnp.float32
    vmem = pl.BlockSpec(memory_space=pltpu.VMEM)
    shapes = [(2, 14, 48, LANES), (10, 32, LANES), (7, 3, 16, LANES), (7, 3, 2, 24, LANES)]
    dma = pltpu.SemaphoreType.DMA
    blocks = 2 * len(NEAR) + 6
    extended = pl.pallas_call(
        exchange,
        out_shape=[jax.ShapeDtypeStruct(shape, f32) for shape in shapes],
        in_specs=[vmem],
        out_specs=[vmem] * 4,
        scratch_shapes=[
            pltpu.VMEM((2, 4, 16, LANES), f32),
            pltpu.VMEM((2, 2, 8, LANES), f32),
            pltpu.VMEM((2, 8, LANES), f32),
            pltpu.VMEM((2, 24, LANES), f32),
            dma((10,)),
            dma((10,)),
            dma((blocks,)),
            dma((blocks,)),
            dma((10,)),
            dma((10,)),
        ],
        compiler_params=pltpu.CompilerParams(collective_id=0, has_side_effects=True, vmem_limit_bytes=16 * 1024 * 1024),
    )(jnp.stack([right_side, reaction]))
    block = jax.ShapeDtypeStruct(right_side.shape, f32)
    spread = []
    for level in (0, 1, 2):
        n = DEPTH[level + 1] + 2
        spread.append(pltpu.VMEM((n, TALL[level + 1], LANES), f32))
        spread.append(pltpu.VMEM((n, 2 if level == 0 else 1, TALL[level], LANES), f32))
    return pl.pallas_call(
        cycle,
        out_shape=[block, block],
        in_specs=[vmem] * 4,
        out_specs=[vmem] * 2,
        scratch_shapes=spread,
        compiler_params=pltpu.CompilerParams(vmem_limit_bytes=16 * 1024 * 1024),
    )(*extended)


def solution(mesh):
    spec = P(*AXES)
    return jax.shard_map(
        lambda s, c: tuple(per_device(s, c)),
        mesh=mesh,
        in_specs=(spec, spec),
        out_specs=(spec, spec),
        check_vma=False,
    )
```
